1024 devices in a mesh: gx: 256 (over y, z, core), gy: 4 (over x).
Axes of the slice: x: 4, y: 8, z: 16, core: 2. Of those that a mesh axis runs over, the one named last changes fastest.
Arguments:
- rhs: float32 [256, 8, 4, 1024], P('gx', 'gy'), may hold values from -4 to 4
- blocks: float32 [256, 8, 4, 7, 4096], P('gx', 'gy'), may hold values from -0.5 to 0.5
Outputs:
- basis_out: float32 [5, 256, 8, 4, 1024], P(None, 'gx', 'gy')
- factor_out: float32 [80, 80], replicated
The draws below stay inside these ranges and needn't reach their ends.
All inputs are finite; a program needn't handle non-finite values.
Results may differ from the reference program's by a relative error of at most 0.0003.
Values sent between devices are 32-bit elements; how exact they have to be, the bound alone decides.
A program may use at most 32 MiB of HBM per device.

```python
import math
import jax
import jax.numpy as jnp
from jax import lax

DOF = 64
RHS = 16
POWERS = 4
COLS = 80
NX = 256
NY = 8
NZ = 4


def draw_rhs(key, part):
    key = jax.random.fold_in(key, 11)
    shared_key, private_key = jax.random.split(key, 2)
    shared_part = jax.random.normal(shared_key, (NX, NY, NZ, DOF, 1), jnp.float32)
    private_part = jax.random.normal(private_key, (NX, NY, NZ, DOF, RHS), jnp.float32)
    spread = 0.7
    mixed = (shared_part + spread * private_part) / math.sqrt(1.0 + spread * spread)
    return jnp.clip(mixed, -4.0, 4.0).reshape(NX, NY, NZ, DOF * RHS)


def steps_of(key, extent, pieces, least, largest):
    factor_of = 1.0
    for position, shards_of in pieces:
        draws = jax.random.uniform(jax.random.fold_in(jax.random.fold_in(key, 6), position), (shards_of,), jnp.float32, least / len(pieces), largest / len(pieces))
        factor_of = factor_of * jnp.repeat(jnp.exp(draws), extent[position] // shards_of).reshape((-1,) + (1,) * (len(extent) - 1 - position))
    return factor_of


def centred(own_key, extent, scale, most, pieces=(), kind=jnp.bfloat16):
    array = jax.random.normal(own_key, extent, jnp.float32) * scale
    if len(pieces) > 0:
        array = steps_of(own_key, extent, pieces, -0.22, 0.18) * array
    return jnp.clip(array, min=-most, max=most).astype(kind)


def setup_inputs(seed: int = 0) -> dict:
    arg_keys = jax.random.split(jax.random.key(seed), 3)
    rhs = draw_rhs(jax.random.fold_in(arg_keys[2], 71), 0)
    blocks = centred(arg_keys[1], (NX, NY, NZ, 7, DOF * DOF), (0.8 / (7 * DOF) ** 0.5), 0.5, ((0, 256), (1, 4)), jnp.float32)
    return dict(rhs=rhs, blocks=blocks)


precise = lax.Precision.HIGHEST

def apply_operator(matrices, vector):
    padded = jnp.pad(vector, ((1, 1), (1, 1), (1, 1), (0, 0), (0, 0)))
    neighbours = [vector, padded[:-2, 1:-1, 1:-1], padded[2:, 1:-1, 1:-1], padded[1:-1, :-2, 1:-1], padded[1:-1, 2:, 1:-1], padded[1:-1, 1:-1, :-2], padded[1:-1, 1:-1, 2:]]
    summed = vector
    for face in range(7):
        summed = summed + jnp.einsum('abcij,abcjr->abcir', matrices[:, :, :, face], neighbours[face], precision=precise)
    return summed

def gram_of(krylov):
    return jnp.einsum('kxr,lxs->krls', krylov, krylov, precision=precise).reshape(COLS, COLS)

def upper_factor(gram_matrix):
    order = gram_matrix.shape[0]
    index_rows = lax.broadcasted_iota(jnp.int32, (order,), 0)
    index_cols = lax.broadcasted_iota(jnp.int32, (order, order), 1)

    def one_column(column, carry):
        remain, lower = carry
        column_vec = lax.dynamic_slice_in_dim(remain, column, 1, 1)[:, 0]
        pivot = jnp.sqrt(lax.dynamic_slice_in_dim(column_vec, column, 1, 0)[0])
        scaled = jnp.where(index_rows >= column, column_vec / pivot, jnp.zeros_like(column_vec))
        lower = jnp.where(index_cols == column, scaled[:, None], lower)
        remain = remain - scaled[:, None] * scaled[None, :]
        return (remain, lower)
    start = (gram_matrix, jnp.zeros_like(gram_matrix))
    remain, lower = lax.fori_loop(0, order, one_column, start)
    return lower.T

def upper_inverse(factor):
    order = factor.shape[0]
    index_rows = lax.broadcasted_iota(jnp.int32, (order, order), 0)
    index_vec = lax.broadcasted_iota(jnp.int32, (order,), 0)

    def one_row(step, solved):
        row = order - 1 - step
        factor_row = lax.dynamic_slice_in_dim(factor, row, 1, 0)[0]
        pivot = lax.dynamic_slice_in_dim(factor_row, row, 1, 0)[0]
        unit_row = jnp.where(index_vec == row, jnp.ones_like(factor_row), jnp.zeros_like(factor_row))
        new_row = (unit_row - jnp.dot(factor_row, solved, precision=precise)) / pivot
        return jnp.where(index_rows == row, new_row[None, :], solved)
    return lax.fori_loop(0, order, one_row, jnp.zeros_like(factor))

def apply_inverse(krylov, factor):
    inverse = upper_inverse(factor)
    return jnp.einsum('lxs,lskr->kxr', krylov, inverse.reshape(POWERS + 1, RHS, POWERS + 1, RHS), precision=precise)

def reference(rhs, blocks):
    matrices = blocks.reshape(NX, NY, NZ, 7, DOF, DOF)
    vector = rhs.reshape(NX, NY, NZ, DOF, RHS)
    collected = [vector]
    for power_index in range(POWERS):
        vector = apply_operator(matrices, vector)
        collected.append(vector)
    krylov = jnp.stack(collected).reshape(POWERS + 1, NX * NY * NZ * DOF, RHS)
    first_r = upper_factor(gram_of(krylov))
    first_q = apply_inverse(krylov, first_r)
    second_r = upper_factor(gram_of(first_q))
    second_q = apply_inverse(first_q, second_r)
    basis_out = second_q.reshape(POWERS + 1, NX, NY, NZ, DOF * RHS)
    factor_out = jnp.dot(second_r, first_r, precision=precise)
    return (basis_out, factor_out)
```

```python
import functools

import jax
import jax.numpy as jnp
from jax import lax
from jax.experimental import pallas as pl
from jax.experimental.pallas import tpu as pltpu
from jax.sharding import PartitionSpec as P

DOF = 64
RHS = 16
POWERS = 4
COLS = 80
ELEMS = 8
LANES = 128
F32 = jnp.float32
BF16 = jnp.bfloat16
PAIRS = ((0, 5), (6, None), (1, 2), (3, 4))


def lane(shape):
    return lax.broadcasted_iota(jnp.int32, shape, len(shape) - 1)


def row(shape):
    return lax.broadcasted_iota(jnp.int32, shape, 0)


def split(a):
    high = a.astype(BF16)
    rest = a - high.astype(F32)
    mid = rest.astype(BF16)
    low = (rest - mid.astype(F32)).astype(BF16)
    return high, mid, low


def dot(a, b, dims=((1,), (0,))):
    return lax.dot_general(a, b, (dims, ((), ())), preferred_element_type=F32)


def dot_exact(a, b, dims=((1,), (0,))):
    return lax.dot_general(
        a, b, (dims, ((), ())), precision=lax.Precision.HIGHEST, preferred_element_type=F32
    )


def transpose_groups(a):
    rows, group = row(a.shape) % 8, lane(a.shape) // 16
    count = a.shape[0]
    for bit in (1, 2, 4):
        up = pltpu.roll(pltpu.roll(a, bit, 0), LANES - 16 * bit, 1)
        down = pltpu.roll(pltpu.roll(a, count - bit, 0), 16 * bit, 1)
        r, g = (rows // bit) % 2, (group // bit) % 2
        a = jnp.where(r == g, a, jnp.where(r == 1, up, down))
    return a


def transpose_arrays(arrays):
    group = lane((DOF, LANES)) // 16
    arrays = list(arrays)
    for bit in (1, 2, 4):
        g = (group // bit) % 2
        out = []
        for place in range(8):
            other = arrays[place ^ bit]
            here = arrays[place]
            if (place // bit) % 2:
                out.append(jnp.where(g == 1, here, pltpu.roll(other, LANES - 16 * bit, 1)))
            else:
                out.append(jnp.where(g == 0, here, pltpu.roll(other, 16 * bit, 1)))
        arrays = out
    return arrays


def bcast_lane(a, index):
    return jnp.broadcast_to(a[:, index : index + 1], (8, LANES))


def bcast_row(a, index):
    return jnp.broadcast_to(a[index : index + 1, :], (8, LANES))


def eliminate(a_ref, w_ref):
    tiles = COLS // 8

    def panel(p, _):
        start = pl.multiple_of(8 * p, 8)
        shift = lax.rem(LANES - 8 * p, LANES)
        a_p, w_p = a_ref[pl.ds(start, 8), :], w_ref[pl.ds(start, 8), :]
        near = pltpu.roll(a_p, shift, 1)
        column = [bcast_lane(near, j) for j in range(8)]
        a = [[bcast_row(column[j], m) for j in range(m + 1)] for m in range(8)]
        inv = [None] * 8
        for j in range(8):
            inv[j] = lax.rsqrt(a[j][j])
            for m in range(j + 1, 8):
                a[m][j] = a[m][j] * inv[j]
            for m in range(j + 1, 8):
                for n in range(j + 1, m + 1):
                    a[m][n] = a[m][n] - a[m][j] * a[n][j]
        li = [[None] * 8 for _ in range(8)]
        for j in range(8):
            li[j][j] = inv[j]
            for i in range(j + 1, 8):
                total = a[i][j] * li[j][j]
                for k in range(j + 1, i):
                    total = total + a[i][k] * li[k][j]
                li[i][j] = -inv[i] * total

        def apply(vectors):
            out = []
            for m in range(8):
                total = li[m][0] * vectors[0]
                for j in range(1, m + 1):
                    total = total + li[m][j] * vectors[j]
                out.append(total)
            return out

        r = apply([bcast_row(a_p, j) for j in range(8)])
        w = apply([bcast_row(w_p, j) for j in range(8)])
        for i in range(tiles):
            a_i, w_i = a_ref[8 * i : 8 * i + 8, :], w_ref[8 * i : 8 * i + 8, :]
            at = pltpu.roll(a_i, shift, 1)
            c = apply([bcast_lane(at, j) for j in range(8)])
            a_n, w_n = a_i, w_i
            for m in range(8):
                a_n = a_n - c[m] * r[m]
                w_n = w_n - c[m] * w[m]
            later = i > p
            a_ref[8 * i : 8 * i + 8, :] = jnp.where(later, a_n, a_i)
            w_ref[8 * i : 8 * i + 8, :] = jnp.where(later, w_n, w_i)
        rows = row((8, LANES))
        r_p, w_q = r[0], w[0]
        for m in range(1, 8):
            r_p = jnp.where(rows == m, r[m], r_p)
            w_q = jnp.where(rows == m, w[m], w_q)
        a_ref[pl.ds(start, 8), :] = jnp.where(lane((8, LANES)) >= rows + start, r_p, 0.0)
        w_ref[pl.ds(start, 8), :] = w_q
        return 0

    lax.fori_loop(0, tiles, panel, 0)


def kernel(sizes, rhs_ref, blocks_ref, basis_ref, factor_ref, raw, flat, b_f32, b_parts, vecs, ypack, hx, hy,
           u_ref, packed, stage_a, stage_b, stage_c, sum_a, sum_b, sum_c, gathered, a_ref, w_ref, r_ref,
           load_sem, hsend, hrecv, asend, arecv):
    ny, nz, nc, nx = sizes
    gx, gy = ny * nz * nc, nx
    me_x, me_y = lax.axis_index("gx"), lax.axis_index("gy")
    core, chip = lax.rem(me_x, nc), lax.div(me_x, nc)
    at_z, at_y = lax.rem(chip, nz), lax.div(chip, nz)

    def place(y, z, c, x):
        return {"gx": (y * nz + z) * nc + c, "gy": x}

    me_g = me_y * nc + core
    n_g = nx * nc

    def mate_g(i):
        return place(at_y, at_z, lax.rem(i, nc), lax.div(i, nc))

    def mate_y(i):
        return place(i, at_z, core, me_y)

    def mate_z(i):
        return place(at_y, i, core, me_y)

    groups = ((n_g, me_g, mate_g), (ny, at_y, mate_y), (nz, at_z, mate_z))
    near = (
        {"gx": lax.rem(me_x + gx - 1, gx), "gy": me_y},
        {"gx": lax.rem(me_x + 1, gx), "gy": me_y},
        {"gx": me_x, "gy": lax.rem(me_y + gy - 1, gy)},
        {"gx": me_x, "gy": lax.rem(me_y + 1, gy)},
    )

    loads = [
        pltpu.make_async_copy(rhs_ref, flat, load_sem.at[0]),
        pltpu.make_async_copy(blocks_ref, raw, load_sem.at[1]),
    ]
    for load in loads:
        load.start()
    barrier = pltpu.get_barrier_semaphore()
    count = 0
    for peer in near:
        pl.semaphore_signal(barrier, inc=1, device_id=peer, device_id_type=pl.DeviceIdType.MESH)
        count += 1
    for n, me, mate in groups:

        @pl.loop(1, n)
        def _(d):
            pl.semaphore_signal(
                barrier, inc=1, device_id=mate(lax.rem(me + d, n)), device_id_type=pl.DeviceIdType.MESH
            )

        count += n - 1

    loads[0].wait()
    flat_rhs = jnp.concatenate([flat[0], flat[1]], axis=0)
    first = jnp.concatenate([flat_rhs[:, LANES * t : LANES * (t + 1)] for t in range(8)], axis=0)
    lanes = lane((DOF, LANES))
    half = lane((DOF // 2, LANES)) < 64

    def remote(src, dst, send, recv, peer):
        return pltpu.make_async_remote_copy(
            src_ref=src, dst_ref=dst, send_sem=send, recv_sem=recv,
            device_id=peer, device_id_type=pl.DeviceIdType.MESH,
        )

    def exchanges(k):
        return (
            remote(vecs.at[k], hx.at[k, 1], hsend.at[k, 0], hrecv.at[k, 0], near[0]),
            remote(vecs.at[k], hx.at[k, 0], hsend.at[k, 1], hrecv.at[k, 1], near[1]),
            remote(ypack.at[k, 0], hy.at[k, 1], hsend.at[k, 2], hrecv.at[k, 2], near[2]),
            remote(ypack.at[k, 1], hy.at[k, 0], hsend.at[k, 3], hrecv.at[k, 3], near[3]),
        )

    def publish(k, v):
        vecs[k] = v
        low, high = v[: DOF // 2], pltpu.roll(v[DOF // 2 :], 64, 1)
        ypack[k, 0] = jnp.where(half, low, high)
        ypack[k, 1] = jnp.where(half, high, low)

    v = transpose_groups(first)
    publish(0, v)
    pl.semaphore_wait(barrier, count)
    sends = [exchanges(0)]
    for copy in sends[0]:
        copy.start()

    loads[1].wait()
    zero8 = jnp.zeros((8, LANES), F32)
    half8 = lane((8, LANES)) < 64

    @pl.loop(0, DOF // 2)
    def _(t):
        at = pl.multiple_of(t * LANES, LANES)

        def face(f):
            if f is None:
                return zero8
            return jnp.concatenate([raw[f, :, pl.ds(at, LANES)], raw[7 + f, :, pl.ds(at, LANES)]], axis=0)

        for place_, (one, two) in enumerate(PAIRS):
            a, b = face(one), face(two)
            b_f32[place_, pl.ds(2 * t, 8, stride=DOF), :] = jnp.where(half8, a, pltpu.roll(b, 64, 1))
            b_f32[place_, pl.ds(2 * t + 1, 8, stride=DOF), :] = jnp.where(half8, pltpu.roll(a, 64, 1), b)

    for place_ in range(4):
        for part, value in enumerate(split(b_f32[place_])):
            b_parts[part, :, LANES * place_ : LANES * (place_ + 1)] = value

    def product(place_, vectors):
        high, mid, low = split(jnp.concatenate(vectors, axis=0))
        both = jnp.concatenate([high, mid], axis=1)
        columns = slice(256 * place_, 256 * (place_ + 1))
        b_high, b_mid, b_low = (b_parts[part, :, columns] for part in range(3))
        wide = dot(b_high, both) + dot(b_mid, both)
        return wide[:, :LANES] + wide[:, LANES:] + (dot(b_high, low) + dot(b_low, high))

    def of_element(a):
        out = jnp.zeros((DOF, LANES), F32)
        for e in range(ELEMS):
            out = jnp.where(lanes // 16 == e, a[DOF * e : DOF * (e + 1)], out)
        return out

    at_cell = (lanes // 16) % 4
    zero = jnp.zeros((DOF, LANES), F32)
    for k in range(POWERS):
        z_low = jnp.where(at_cell == 0, 0.0, pltpu.roll(v, 16, 1))
        z_high = jnp.where(at_cell == 3, 0.0, pltpu.roll(v, LANES - 16, 1))
        inner = product(0, [v, z_low, z_high, zero])
        swapped = pltpu.roll(v, 64, 1)
        for copy in sends[k]:
            copy.wait_recv()
        x_low = jnp.where(me_x > 0, hx[k, 0], 0.0)
        x_high = jnp.where(me_x < gx - 1, hx[k, 1], 0.0)
        y_low = jnp.where(me_y > 0, hy[k, 0], 0.0)
        y_high = jnp.where(me_y < gy - 1, hy[k, 1], 0.0)
        own_low, own_high = swapped[: DOF // 2], swapped[DOF // 2 :]
        y_low = jnp.concatenate(
            [jnp.where(half, pltpu.roll(y_low, 64, 1), own_low), jnp.where(half, y_low, own_high)], axis=0
        )
        y_high = jnp.concatenate(
            [jnp.where(half, own_low, pltpu.roll(y_high, 64, 1)), jnp.where(half, own_high, y_high)], axis=0
        )
        outer = product(1, [x_low, x_high, y_low, y_high])
        v = v + of_element(inner + outer)
        if k < POWERS - 1:
            publish(k + 1, v)
            sends.append(exchanges(k + 1))
            for copy in sends[k + 1]:
                copy.start()
        else:
            vecs[POWERS] = v

    columns = transpose_arrays([vecs[k] for k in range(POWERS + 1)] + [zero] * (7 - POWERS))
    for e in range(ELEMS):
        u_ref[DOF * e : DOF * (e + 1), :] = columns[e]

    def all_bytes(buffer, n, sem):
        return pltpu.make_async_copy(buffer.at[pl.ds(0, n - 1)], buffer.at[pl.ds(0, n - 1)], sem)

    def add_up(buffer, n):
        total = buffer[0]
        for i in range(1, n):
            total = total + buffer[i]
        return total

    def one_pass(number, _):
        u = u_ref[...]
        gram = dot_exact(u, u, ((0,), (0,)))[:COLS]
        def block(k, to):
            part = gram[RHS * k : RHS * (k + 1)]
            return pltpu.roll(part, (to - RHS * k) % LANES, 1) if (to - RHS * k) % LANES else part

        lane16 = lane((RHS, LANES))
        top = jnp.where(lane16 < 80, block(0, 0), block(2, 80))
        low = jnp.where(lane16 < 64, block(1, 0), jnp.where(lane16 < 96, block(3, 64), block(4, 96)))
        both = jnp.concatenate([top, low], axis=0)
        piece = 2 * RHS // n_g
        for i in range(n_g):
            packed[number, i] = both[piece * i : piece * (i + 1)]

        def start_all(n, me, mate, src, dst, sem):
            @pl.loop(1, n)
            def _(d):
                other = lax.rem(me + d, n)
                remote(src(other), dst, asend.at[number, sem], arecv.at[number, sem], mate(other)).start()

        start_all(n_g, me_g, mate_g, lambda i: packed.at[number, i], stage_a.at[number, me_g], 0)
        stage_a[number, me_g] = packed[number, me_g]
        all_bytes(stage_a.at[number], n_g, arecv.at[number, 0]).wait()
        sum_a[number] = add_up(stage_a.at[number], n_g)
        start_all(ny, at_y, mate_y, lambda i: sum_a.at[number], stage_b.at[number, at_y], 1)
        stage_b[number, at_y] = sum_a[number]
        all_bytes(stage_b.at[number], ny, arecv.at[number, 1]).wait()
        sum_b[number] = add_up(stage_b.at[number], ny)
        start_all(nz, at_z, mate_z, lambda i: sum_b.at[number], stage_c.at[number, at_z], 2)
        stage_c[number, at_z] = sum_b[number]
        all_bytes(stage_c.at[number], nz, arecv.at[number, 2]).wait()
        sum_c[number] = add_up(stage_c.at[number], nz)
        start_all(n_g, me_g, mate_g, lambda i: sum_c.at[number], gathered.at[number, me_g], 3)
        gathered[number, me_g] = sum_c[number]
        all_bytes(gathered.at[number], n_g, arecv.at[number, 3]).wait()

        both = jnp.concatenate([gathered[number, i] for i in range(n_g)], axis=0)
        top, low = both[:RHS], both[RHS:]
        blocks_of = (
            (top, 0, 80), (low, 0, 64), (top, 80, 48), (low, 64, 32), (low, 96, 16)
        )
        upper = []
        for k, (source, at, width) in enumerate(blocks_of):
            shift = (RHS * k - at) % LANES
            part = pltpu.roll(source, shift, 1) if shift else source
            upper.append(jnp.where((lane16 >= RHS * k) & (lane16 < COLS), part, 0.0))
        upper = jnp.concatenate(upper + [jnp.zeros((LANES - COLS, LANES), F32)], axis=0)
        r_, c_ = row((LANES, LANES)), lane((LANES, LANES))
        full = jnp.where(r_ // RHS <= c_ // RHS, upper, upper.T)
        a_ref[...] = full[:COLS]
        w_ref[...] = (r_ == c_).astype(F32)[:COLS]
        eliminate(a_ref, w_ref)
        r_ref[number] = a_ref[...]
        inverse = jnp.concatenate([w_ref[...], jnp.zeros((LANES - COLS, LANES), F32)], axis=0)
        u_ref[...] = dot_exact(u, inverse, ((1,), (1,)))
        return 0

    lax.fori_loop(0, 2, one_pass, 0)

    pad = jnp.zeros((LANES - COLS, LANES), F32)
    factor = dot_exact(r_ref[1], jnp.concatenate([r_ref[0], pad], axis=0))
    factor_ref[...] = factor[:, :COLS]
    columns = transpose_arrays([u_ref[DOF * e : DOF * (e + 1), :] for e in range(ELEMS)])
    for k in range(POWERS + 1):
        out = transpose_groups(columns[k])
        for t in range(8):
            at = slice(LANES * t, LANES * (t + 1))
            basis_ref[k, 0, :, at] = out[8 * t : 8 * t + 4]
            basis_ref[k, 1, :, at] = out[8 * t + 4 : 8 * t + 8]

    for copies in sends:
        for copy in copies:
            copy.wait_send()
    for number in range(2):
        all_bytes(stage_a.at[number], n_g, asend.at[number, 0]).wait()
        all_bytes(stage_b.at[number], ny, asend.at[number, 1]).wait()
        all_bytes(stage_c.at[number], nz, asend.at[number, 2]).wait()
        all_bytes(gathered.at[number], n_g, asend.at[number, 3]).wait()


def on_device(sizes, rhs, blocks):
    ny, nz, nc, nx = sizes
    n_g = nx * nc
    piece = 2 * RHS // n_g
    faces = blocks.transpose(0, 1, 3, 2, 4).reshape(14, 4, DOF * DOF)
    vmem = pltpu.VMEM
    basis, factor = pl.pallas_call(
        functools.partial(kernel, sizes),
        out_shape=(
            jax.ShapeDtypeStruct((POWERS + 1, 2, 4, DOF * RHS), F32),
            jax.ShapeDtypeStruct((COLS, COLS), F32),
        ),
        in_specs=[pl.BlockSpec(memory_space=pl.ANY)] * 2,
        out_specs=(pl.BlockSpec(memory_space=pltpu.VMEM),) * 2,
        scratch_shapes=[
            vmem((14, 4, DOF * DOF), F32),
            vmem((2, 4, DOF * RHS), F32),
            vmem((4, ELEMS * DOF, LANES), F32),
            vmem((3, ELEMS * DOF, 4 * LANES), BF16),
            vmem((POWERS + 1, DOF, LANES), F32),
            vmem((POWERS, 2, DOF // 2, LANES), F32),
            vmem((POWERS, 2, DOF, LANES), F32),
            vmem((POWERS, 2, DOF // 2, LANES), F32),
            vmem((ELEMS * DOF, LANES), F32),
            vmem((2, n_g, piece, LANES), F32),
            vmem((2, n_g, piece, LANES), F32),
            vmem((2, ny, piece, LANES), F32),
            vmem((2, nz, piece, LANES), F32),
            vmem((2, piece, LANES), F32),
            vmem((2, piece, LANES), F32),
            vmem((2, piece, LANES), F32),
            vmem((2, n_g, piece, LANES), F32),
            vmem((COLS, LANES), F32),
            vmem((COLS, LANES), F32),
            vmem((2, COLS, LANES), F32),
            pltpu.SemaphoreType.DMA((2,)),
            pltpu.SemaphoreType.DMA((POWERS, 4)),
            pltpu.SemaphoreType.DMA((POWERS, 4)),
            pltpu.SemaphoreType.DMA((2, 4)),
            pltpu.SemaphoreType.DMA((2, 4)),
        ],
        compiler_params=pltpu.CompilerParams(
            collective_id=0, has_side_effects=True, vmem_limit_bytes=40 * 1024 * 1024
        ),
        name="krylov_qr",
    )(rhs.reshape(2, 4, DOF * RHS), faces)
    return basis.reshape(POWERS + 1, 1, 2, 4, DOF * RHS), factor


def solution(mesh):
    gx, gy = mesh.shape["gx"], mesh.shape["gy"]
    nz = 16 if gx >= 64 else 2
    return jax.shard_map(
        functools.partial(on_device, (gx // (2 * nz), nz, 2, gy)),
        mesh=mesh,
        in_specs=(P("gx", "gy", None, None), P("gx", "gy", None, None, None)),
        out_specs=(P(None, "gx", "gy", None, None), P()),
        check_vma=False,
    )
```

```python
import functools

import jax
import jax.numpy as jnp
from jax import lax
from jax.experimental import pallas as pl
from jax.experimental.pallas import tpu as pltpu
from jax.sharding import PartitionSpec as P

DOF = 64
RHS = 16
POWERS = 4
COLS = 80
ELEMS = 8
LANES = 128
F32 = jnp.float32
BF16 = jnp.bfloat16
PAIRS = ((0, 5), (6, None), (1, 2), (3, 4))


def lane(shape):
    return lax.broadcasted_iota(jnp.int32, shape, len(shape) - 1)


def row(shape):
    return lax.broadcasted_iota(jnp.int32, shape, 0)


def split(a):
    high = a.astype(BF16)
    rest = a - high.astype(F32)
    mid = rest.astype(BF16)
    low = (rest - mid.astype(F32)).astype(BF16)
    return high, mid, low


def dot(a, b, dims=((1,), (0,))):
    return lax.dot_general(a, b, (dims, ((), ())), preferred_element_type=F32)


def dot_exact(a, b, dims=((1,), (0,))):
    return lax.dot_general(
        a, b, (dims, ((), ())), precision=lax.Precision.HIGHEST, preferred_element_type=F32
    )


def transpose_groups(a):
    rows, group = row(a.shape) % 8, lane(a.shape) // 16
    count = a.shape[0]
    for bit in (1, 2, 4):
        up = pltpu.roll(pltpu.roll(a, bit, 0), LANES - 16 * bit, 1)
        down = pltpu.roll(pltpu.roll(a, count - bit, 0), 16 * bit, 1)
        r, g = (rows // bit) % 2, (group // bit) % 2
        a = jnp.where(r == g, a, jnp.where(r == 1, up, down))
    return a


def transpose_arrays(arrays):
    group = lane((DOF, LANES)) // 16
    arrays = list(arrays)
    for bit in (1, 2, 4):
        g = (group // bit) % 2
        out = []
        for place in range(8):
            other = arrays[place ^ bit]
            here = arrays[place]
            if (place // bit) % 2:
                out.append(jnp.where(g == 1, here, pltpu.roll(other, LANES - 16 * bit, 1)))
            else:
                out.append(jnp.where(g == 0, here, pltpu.roll(other, 16 * bit, 1)))
        arrays = out
    return arrays


def pick(a, index):
    return a[index : index + 1, :]


def spread(a, index):
    return jnp.broadcast_to(a[:, index : index + 1], a.shape)


def stacked(rows):
    at = row((8, LANES))
    out = jnp.broadcast_to(rows[0], (8, LANES))
    for m in range(1, 8):
        out = jnp.where(at == m, rows[m], out)
    return out


def eliminate(full):
    later = full
    rest = (row((COLS, LANES)) == lane((COLS, LANES))).astype(F32)
    factor, inverse = [], []
    for p in range(COLS // 8):
        start = 8 * p
        at, at_w = later[:8], rest[:8]
        later, rest = later[8:], rest[8:]
        more = p < COLS // 8 - 1
        column = [spread(at, start + j) for j in range(8)]
        r, w = [pick(at, j) for j in range(8)], [pick(at_w, j) for j in range(8)]
        below = [spread(later, start + j) for j in range(8)] if more else None
        for j in range(8):
            inv = lax.rsqrt(pick(column[j], j))
            r[j], w[j] = r[j] * inv, w[j] * inv
            scaled = column[j] * inv
            for m in range(j + 1, 8):
                s = pick(scaled, m)
                column[m] = column[m] - scaled * s
                r[m], w[m] = r[m] - s * r[j], w[m] - s * w[j]
            if more:
                below[j] = below[j] * inv
                for m in range(j + 1, 8):
                    below[m] = below[m] - below[j] * pick(scaled, m)
                later = later - below[j] * r[j]
                rest = rest - below[j] * w[j]
        upper = lane((8, LANES)) >= row((8, LANES)) + start
        factor.append(jnp.where(upper, stacked(r), 0.0))
        inverse.append(stacked(w))
    return jnp.concatenate(factor, axis=0), jnp.concatenate(inverse, axis=0)


def kernel(sizes, rhs_ref, blocks_ref, basis_ref, factor_ref, raw, flat, b_f32, b_parts, vecs, ypack, hx, hy,
           u_ref, packed, stage_a, stage_b, stage_c, sum_a, sum_b, sum_c, gathered, r_ref,
           load_sem, hsend, hrecv, asend, arecv, word):
    ny, nz, nc, nx = sizes
    gx, gy = ny * nz * nc, nx
    me_x, me_y = lax.axis_index("gx"), lax.axis_index("gy")
    core, chip = lax.rem(me_x, nc), lax.div(me_x, nc)
    at_z, at_y = lax.rem(chip, nz), lax.div(chip, nz)

    def place(y, z, c, x):
        return {"gx": (y * nz + z) * nc + c, "gy": x}

    me_g = me_y * nc + core
    n_g = nx * nc

    def mate_g(i):
        return place(at_y, at_z, lax.rem(i, nc), lax.div(i, nc))

    def mate_y(i):
        return place(i, at_z, core, me_y)

    def mate_z(i):
        return place(at_y, i, core, me_y)

    groups = ((n_g, me_g, mate_g), (ny, at_y, mate_y), (nz, at_z, mate_z))
    near = (
        {"gx": lax.rem(me_x + gx - 1, gx), "gy": me_y},
        {"gx": lax.rem(me_x + 1, gx), "gy": me_y},
        {"gx": me_x, "gy": lax.rem(me_y + gy - 1, gy)},
        {"gx": me_x, "gy": lax.rem(me_y + 1, gy)},
    )

    loads = [
        pltpu.make_async_copy(rhs_ref, flat, load_sem.at[0]),
        pltpu.make_async_copy(blocks_ref, raw, load_sem.at[1]),
    ]
    for load in loads:
        load.start()
    barrier = pltpu.get_barrier_semaphore()

    def signal(semaphore, peer):
        pl.semaphore_signal(semaphore, inc=1, device_id=peer, device_id_type=pl.DeviceIdType.MESH)

    def at_distance(d):
        peers = []
        for n, me, mate in groups[1:]:
            if d == 1 or 2 * d <= n // 2:
                peers += [mate(lax.rem(me + d, n)), mate(lax.rem(me + n - d, n))]
        return peers

    greeted = list(near) + at_distance(1)
    for peer in greeted:
        signal(barrier, peer)
    for d in range(1, n_g):
        signal(barrier, mate_g(lax.rem(me_g + d, n_g)))
    count = len(greeted) + n_g - 1

    loads[0].wait()
    flat_rhs = jnp.concatenate([flat[0], flat[1]], axis=0)
    first = jnp.concatenate([flat_rhs[:, LANES * t : LANES * (t + 1)] for t in range(8)], axis=0)
    lanes = lane((DOF, LANES))
    half = lane((DOF // 2, LANES)) < 64

    def remote(src, dst, send, recv, peer):
        return pltpu.make_async_remote_copy(
            src_ref=src, dst_ref=dst, send_sem=send, recv_sem=recv,
            device_id=peer, device_id_type=pl.DeviceIdType.MESH,
        )

    def exchanges(k):
        return (
            remote(vecs.at[k], hx.at[k, 1], hsend.at[k, 0], hrecv.at[k, 0], near[0]),
            remote(vecs.at[k], hx.at[k, 0], hsend.at[k, 1], hrecv.at[k, 1], near[1]),
            remote(ypack.at[k, 0], hy.at[k, 1], hsend.at[k, 2], hrecv.at[k, 2], near[2]),
            remote(ypack.at[k, 1], hy.at[k, 0], hsend.at[k, 3], hrecv.at[k, 3], near[3]),
        )

    def publish(k, v):
        vecs[k] = v
        low, high = v[: DOF // 2], pltpu.roll(v[DOF // 2 :], 64, 1)
        ypack[k, 0] = jnp.where(half, low, high)
        ypack[k, 1] = jnp.where(half, high, low)

    zero8 = jnp.zeros((8, LANES), F32)
    half8 = lane((8, LANES)) < 64

    def prepare(places):
        @pl.loop(0, DOF // 8)
        def _(quad):
            for step in range(4):
                t = 4 * quad + step
                at = pl.multiple_of(t * LANES, LANES)

                def face(f):
                    if f is None:
                        return zero8
                    return jnp.concatenate([raw[f, :, pl.ds(at, LANES)], raw[7 + f, :, pl.ds(at, LANES)]], axis=0)

                for place_ in places:
                    one, two = PAIRS[place_]
                    a, b = face(one), face(two)
                    b_f32[place_, pl.ds(2 * t, 8, stride=DOF), :] = jnp.where(half8, a, pltpu.roll(b, 64, 1))
                    b_f32[place_, pl.ds(2 * t + 1, 8, stride=DOF), :] = jnp.where(half8, pltpu.roll(a, 64, 1), b)

        for i, place_ in enumerate(places):
            high, mid, low = split(b_f32[place_])
            for part, value in enumerate((mid, high, low)):
                at = 2 * LANES * part + LANES * i
                b_parts[places[0] // 2, :, at : at + LANES] = value

    v = transpose_groups(first)
    publish(0, v)
    loads[1].wait()
    prepare((0, 1))
    pl.semaphore_wait(barrier, count)
    sends = [exchanges(0)]
    for copy in sends[0]:
        copy.start()
    prepare((2, 3))

    def product(which, vectors):
        high, mid, low = split(jnp.concatenate(vectors, axis=0))
        both = jnp.concatenate([high, mid], axis=1)
        wide = dot(b_parts[which, :, : 4 * LANES], jnp.concatenate([both, both], axis=0))
        rest = dot(b_parts[which, :, 2 * LANES :], jnp.concatenate([low, high], axis=0))
        total = wide[:, :LANES] + wide[:, LANES:] + rest
        out = total[:DOF]
        for e in range(1, ELEMS):
            out = jnp.where(lanes // 16 == e, total[DOF * e : DOF * (e + 1)], out)
        return out

    known = [at_distance(d) for d in (1, 2, 4) if 2 * d <= max(ny, nz) // 2]
    at_cell = (lanes // 16) % 4
    zero = jnp.zeros((DOF, LANES), F32)
    for k in range(POWERS):
        z_low = jnp.where(at_cell == 0, 0.0, pltpu.roll(v, 16, 1))
        z_high = jnp.where(at_cell == 3, 0.0, pltpu.roll(v, LANES - 16, 1))
        inner = v + product(0, [v, z_low, z_high, zero])
        swapped = pltpu.roll(v, 64, 1)
        if k < len(known):
            for peer in known[k]:
                signal(word.at[k], peer)
        for copy in sends[k]:
            copy.wait_recv()
        x_low = jnp.where(me_x > 0, hx[k, 0], 0.0)
        x_high = jnp.where(me_x < gx - 1, hx[k, 1], 0.0)
        y_low = jnp.where(me_y > 0, hy[k, 0], 0.0)
        y_high = jnp.where(me_y < gy - 1, hy[k, 1], 0.0)
        own_low, own_high = swapped[: DOF // 2], swapped[DOF // 2 :]
        y_low = jnp.concatenate(
            [jnp.where(half, pltpu.roll(y_low, 64, 1), own_low), jnp.where(half, y_low, own_high)], axis=0
        )
        y_high = jnp.concatenate(
            [jnp.where(half, own_low, pltpu.roll(y_high, 64, 1)), jnp.where(half, own_high, y_high)], axis=0
        )
        outer = product(1, [x_low, x_high, y_low, y_high])
        if k < len(known):
            pl.semaphore_wait(word.at[k], len(known[k]))
        v = inner + outer
        if k < POWERS - 1:
            publish(k + 1, v)
            sends.append(exchanges(k + 1))
            for copy in sends[k + 1]:
                copy.start()
        else:
            vecs[POWERS] = v

    columns = transpose_arrays([vecs[k] for k in range(POWERS + 1)] + [zero] * (7 - POWERS))
    for e in range(ELEMS):
        u_ref[DOF * e : DOF * (e + 1), :] = columns[e]

    def all_bytes(buffer, n, sem):
        return pltpu.make_async_copy(buffer.at[pl.ds(0, n - 1)], buffer.at[pl.ds(0, n - 1)], sem)

    def add_up(buffer, n):
        total = buffer[0]
        for i in range(1, n):
            total = total + buffer[i]
        return total

    def one_pass(number, _):
        u = u_ref[...]
        gram = dot_exact(u, u, ((0,), (0,)))[:COLS]
        def block(k, to):
            part = gram[RHS * k : RHS * (k + 1)]
            return pltpu.roll(part, (to - RHS * k) % LANES, 1) if (to - RHS * k) % LANES else part

        lane16 = lane((RHS, LANES))
        top = jnp.where(lane16 < 80, block(0, 0), block(2, 80))
        low = jnp.where(lane16 < 64, block(1, 0), jnp.where(lane16 < 96, block(3, 64), block(4, 96)))
        both = jnp.concatenate([top, low], axis=0)
        piece = 2 * RHS // n_g
        for i in range(n_g):
            packed[number, i] = both[piece * i : piece * (i + 1)]

        def start_all(n, me, mate, src, dst, sem):
            for d in sorted(range(1, n), key=lambda d: -min(d, n - d)):
                other = lax.rem(me + d, n)
                remote(src(other), dst, asend.at[number, sem], arecv.at[number, sem], mate(other)).start()

        start_all(n_g, me_g, mate_g, lambda i: packed.at[number, i], stage_a.at[number, me_g], 0)
        stage_a[number, me_g] = packed[number, me_g]
        all_bytes(stage_a.at[number], n_g, arecv.at[number, 0]).wait()
        sum_a[number] = add_up(stage_a.at[number], n_g)
        start_all(ny, at_y, mate_y, lambda i: sum_a.at[number], stage_b.at[number, at_y], 1)
        stage_b[number, at_y] = sum_a[number]
        all_bytes(stage_b.at[number], ny, arecv.at[number, 1]).wait()
        sum_b[number] = add_up(stage_b.at[number], ny)
        start_all(nz, at_z, mate_z, lambda i: sum_b.at[number], stage_c.at[number, at_z], 2)
        stage_c[number, at_z] = sum_b[number]
        all_bytes(stage_c.at[number], nz, arecv.at[number, 2]).wait()
        sum_c[number] = add_up(stage_c.at[number], nz)
        start_all(n_g, me_g, mate_g, lambda i: sum_c.at[number], gathered.at[number, me_g], 3)
        gathered[number, me_g] = sum_c[number]
        all_bytes(gathered.at[number], n_g, arecv.at[number, 3]).wait()

        both = jnp.concatenate([gathered[number, i] for i in range(n_g)], axis=0)
        top, low = both[:RHS], both[RHS:]
        blocks_of = (
            (top, 0, 80), (low, 0, 64), (top, 80, 48), (low, 64, 32), (low, 96, 16)
        )
        upper = []
        for k, (source, at, width) in enumerate(blocks_of):
            shift = (RHS * k - at) % LANES
            part = pltpu.roll(source, shift, 1) if shift else source
            upper.append(jnp.where((lane16 >= RHS * k) & (lane16 < COLS), part, 0.0))
        upper = jnp.concatenate(upper + [jnp.zeros((LANES - COLS, LANES), F32)], axis=0)
        r_, c_ = row((LANES, LANES)), lane((LANES, LANES))
        full = jnp.where(r_ // RHS <= c_ // RHS, upper, upper.T)
        factor, inverse = eliminate(full[:COLS])
        r_ref[number] = factor
        inverse = jnp.concatenate([inverse, jnp.zeros((LANES - COLS, LANES), F32)], axis=0)
        u_ref[...] = dot_exact(u, inverse, ((1,), (1,)))
        return 0

    lax.fori_loop(0, 2, one_pass, 0)

    pad = jnp.zeros((LANES - COLS, LANES), F32)
    factor = dot_exact(r_ref[1], jnp.concatenate([r_ref[0], pad], axis=0))
    factor_ref[...] = factor[:, :COLS]
    columns = transpose_arrays([u_ref[DOF * e : DOF * (e + 1), :] for e in range(ELEMS)])
    for k in range(POWERS + 1):
        out = transpose_groups(columns[k])
        for t in range(8):
            at = slice(LANES * t, LANES * (t + 1))
            basis_ref[k, 0, :, at] = out[8 * t : 8 * t + 4]
            basis_ref[k, 1, :, at] = out[8 * t + 4 : 8 * t + 8]

    for copies in sends:
        for copy in copies:
            copy.wait_send()
    for number in range(2):
        all_bytes(stage_a.at[number], n_g, asend.at[number, 0]).wait()
        all_bytes(stage_b.at[number], ny, asend.at[number, 1]).wait()
        all_bytes(stage_c.at[number], nz, asend.at[number, 2]).wait()
        all_bytes(gathered.at[number], n_g, asend.at[number, 3]).wait()


def on_device(sizes, rhs, blocks):
    ny, nz, nc, nx = sizes
    n_g = nx * nc
    piece = 2 * RHS // n_g
    faces = blocks.transpose(0, 1, 3, 2, 4).reshape(14, 4, DOF * DOF)
    vmem = pltpu.VMEM
    basis, factor = pl.pallas_call(
        functools.partial(kernel, sizes),
        out_shape=(
            jax.ShapeDtypeStruct((POWERS + 1, 2, 4, DOF * RHS), F32),
            jax.ShapeDtypeStruct((COLS, COLS), F32),
        ),
        in_specs=[pl.BlockSpec(memory_space=pl.ANY)] * 2,
        out_specs=(pl.BlockSpec(memory_space=pltpu.VMEM),) * 2,
        scratch_shapes=[
            vmem((14, 4, DOF * DOF), F32),
            vmem((2, 4, DOF * RHS), F32),
            vmem((4, ELEMS * DOF, LANES), F32),
            vmem((2, ELEMS * DOF, 6 * LANES), BF16),
            vmem((POWERS + 1, DOF, LANES), F32),
            vmem((POWERS, 2, DOF // 2, LANES), F32),
            vmem((POWERS, 2, DOF, LANES), F32),
            vmem((POWERS, 2, DOF // 2, LANES), F32),
            vmem((ELEMS * DOF, LANES), F32),
            vmem((2, n_g, piece, LANES), F32),
            vmem((2, n_g, piece, LANES), F32),
            vmem((2, ny, piece, LANES), F32),
            vmem((2, nz, piece, LANES), F32),
            vmem((2, piece, LANES), F32),
            vmem((2, piece, LANES), F32),
            vmem((2, piece, LANES), F32),
            vmem((2, n_g, piece, LANES), F32),
            vmem((2, COLS, LANES), F32),
            pltpu.SemaphoreType.DMA((2,)),
            pltpu.SemaphoreType.DMA((POWERS, 4)),
            pltpu.SemaphoreType.DMA((POWERS, 4)),
            pltpu.SemaphoreType.DMA((2, 4)),
            pltpu.SemaphoreType.DMA((2, 4)),
            pltpu.SemaphoreType.REGULAR((POWERS,)),
        ],
        compiler_params=pltpu.CompilerParams(
            collective_id=0, has_side_effects=True, vmem_limit_bytes=60 * 1024 * 1024
        ),
        name="krylov_qr",
    )(rhs.reshape(2, 4, DOF * RHS), faces)
    return basis.reshape(POWERS + 1, 1, 2, 4, DOF * RHS), factor


def solution(mesh):
    gx, gy = mesh.shape["gx"], mesh.shape["gy"]
    nz = 16 if gx >= 64 else 2
    return jax.shard_map(
        functools.partial(on_device, (gx // (2 * nz), nz, 2, gy)),
        mesh=mesh,
        in_specs=(P("gx", "gy", None, None), P("gx", "gy", None, None, None)),
        out_specs=(P(None, "gx", "gy", None, None), P()),
        check_vma=False,
    )
```

```python
import functools

import jax
import jax.numpy as jnp
from jax import lax
from jax.experimental import pallas as pl
from jax.experimental.pallas import tpu as pltpu
from jax.sharding import PartitionSpec as P

DOF = 64
RHS = 16
POWERS = 4
COLS = 80
ELEMS = 8
LANES = 128
PANEL = 16
F32 = jnp.float32
BF16 = jnp.bfloat16
PAIRS = ((0, 5), (6, None), (1, 2), (3, 4))


def lane(shape):
    return lax.broadcasted_iota(jnp.int32, shape, len(shape) - 1)


def row(shape):
    return lax.broadcasted_iota(jnp.int32, shape, 0)


def split(a):
    high = a.astype(BF16)
    rest = a - high.astype(F32)
    mid = rest.astype(BF16)
    low = (rest - mid.astype(F32)).astype(BF16)
    return high, mid, low


def dot(a, b, dims=((1,), (0,))):
    return lax.dot_general(a, b, (dims, ((), ())), preferred_element_type=F32)


def dot_exact(a, b, side=1):
    a_high, a_mid, a_low = split(a)
    b_high, b_mid, b_low = split(b)
    both = jnp.concatenate([b_high, b_mid], axis=1)
    dims = ((side,), (0,))
    wide = dot(jnp.concatenate([a_mid, a_high], axis=side), jnp.concatenate([both, both], axis=0), dims)
    rest = dot(jnp.concatenate([a_high, a_low], axis=side), jnp.concatenate([b_low, b_high], axis=0), dims)
    n = b.shape[1]
    return wide[:, :n] + wide[:, n:] + rest


def transpose_groups(a):
    rows, group = row(a.shape) % 8, lane(a.shape) // 16
    count = a.shape[0]
    for bit in (1, 2, 4):
        up = pltpu.roll(pltpu.roll(a, bit, 0), LANES - 16 * bit, 1)
        down = pltpu.roll(pltpu.roll(a, count - bit, 0), 16 * bit, 1)
        r, g = (rows // bit) % 2, (group // bit) % 2
        a = jnp.where(r == g, a, jnp.where(r == 1, up, down))
    return a


def transpose_arrays(arrays):
    group = lane((DOF, LANES)) // 16
    arrays = list(arrays)
    for bit in (1, 2, 4):
        g = (group // bit) % 2
        out = []
        for place in range(8):
            other = arrays[place ^ bit]
            here = arrays[place]
            if (place // bit) % 2:
                out.append(jnp.where(g == 1, here, pltpu.roll(other, LANES - 16 * bit, 1)))
            else:
                out.append(jnp.where(g == 0, here, pltpu.roll(other, 16 * bit, 1)))
        arrays = out
    return arrays


def pick(a, index):
    return a[index : index + 1, :]


def spread(a, index):
    return jnp.broadcast_to(a[:, index : index + 1], a.shape)


def stacked(rows):
    at = row((PANEL, LANES))
    out = jnp.broadcast_to(rows[0], (PANEL, LANES))
    for m in range(1, PANEL):
        out = jnp.where(at == m, rows[m], out)
    return out


def eliminate(full):
    later = full
    upper, diagonal, inverse = [], [], []
    for p in range(COLS // PANEL):
        start = PANEL * p
        more = p < COLS // PANEL - 1
        column = [spread(later[:PANEL], start + j) for j in range(PANEL)]
        below = [spread(later[PANEL:], start + j) for j in range(PANEL)] if more else None
        at = lane(later.shape)
        own = (at >= start) & (at < start + PANEL)
        later = jnp.where(own, (row(later.shape) + start == at).astype(F32), later)
        first, later = later[:PANEL], later[PANEL:]
        r = [pick(first, j) for j in range(PANEL)]
        at = lane((PANEL, LANES))
        corner = jnp.zeros((PANEL, LANES), F32)
        for j in range(PANEL):
            inv = lax.rsqrt(pick(column[j], j))
            r[j] = r[j] * inv
            scaled = column[j] * inv
            corner = jnp.where(at == start + j, scaled, corner)
            for m in range(j + 1, PANEL):
                s = pick(scaled, m)
                column[m] = column[m] - scaled * s
                r[m] = r[m] - s * r[j]
            if more:
                below[j] = below[j] * inv
                for m in range(j + 1, PANEL):
                    below[m] = below[m] - below[j] * pick(scaled, m)
                later = later - below[j] * r[j]
        rows = stacked(r)
        inverse.append(jnp.where(at < start + PANEL, rows, 0.0))
        upper.append(jnp.where(at >= start + PANEL, rows, 0.0))
        diagonal.append(jnp.where(at <= row((PANEL, LANES)) + start, corner, 0.0))
    below = jnp.concatenate(diagonal + [jnp.zeros((LANES - COLS, LANES), F32)], axis=0)
    return jnp.concatenate(upper, axis=0) + below.T[:COLS], jnp.concatenate(inverse, axis=0)


def kernel(sizes, rhs_ref, blocks_ref, basis_ref, factor_ref, raw, b_f32, b_parts, vecs, ypack, hx, hy,
           u_ref, packed, stage_a, stage_b, stage_c, sum_a, sum_b, sum_c, gathered, r_ref,
           load_sem, hsend, hrecv, asend, arecv, word):
    ny, nz, nc, nx = sizes
    gx, gy = ny * nz * nc, nx
    me_x, me_y = lax.axis_index("gx"), lax.axis_index("gy")
    core, chip = lax.rem(me_x, nc), lax.div(me_x, nc)
    at_z, at_y = lax.rem(chip, nz), lax.div(chip, nz)

    def place(y, z, c, x):
        return {"gx": (y * nz + z) * nc + c, "gy": x}

    me_g = me_y * nc + core
    n_g = nx * nc

    def mate_g(i):
        return place(at_y, at_z, lax.rem(i, nc), lax.div(i, nc))

    def mate_y(i):
        return place(i, at_z, core, me_y)

    def mate_z(i):
        return place(at_y, i, core, me_y)

    groups = ((n_g, me_g, mate_g), (ny, at_y, mate_y), (nz, at_z, mate_z))
    near = (
        {"gx": lax.rem(me_x + gx - 1, gx), "gy": me_y},
        {"gx": lax.rem(me_x + 1, gx), "gy": me_y},
        {"gx": me_x, "gy": lax.rem(me_y + gy - 1, gy)},
        {"gx": me_x, "gy": lax.rem(me_y + 1, gy)},
    )

    load = pltpu.make_async_copy(blocks_ref, raw, load_sem.at[0])
    load.start()
    barrier = pltpu.get_barrier_semaphore()

    def signal(semaphore, peer):
        pl.semaphore_signal(semaphore, inc=1, device_id=peer, device_id_type=pl.DeviceIdType.MESH)

    def at_distance(d):
        peers = []
        for n, me, mate in groups[1:]:
            if d == 1 or 2 * d <= n // 2:
                peers += [mate(lax.rem(me + d, n)), mate(lax.rem(me + n - d, n))]
        return peers

    greeted = list(near) + at_distance(1)
    for peer in greeted:
        signal(barrier, peer)
    for d in range(1, n_g):
        signal(barrier, mate_g(lax.rem(me_g + d, n_g)))
    count = len(greeted) + n_g - 1

    flat_rhs = jnp.concatenate([rhs_ref[0], rhs_ref[1]], axis=0)
    first = jnp.concatenate([flat_rhs[:, LANES * t : LANES * (t + 1)] for t in range(8)], axis=0)
    lanes = lane((DOF, LANES))
    half = lane((DOF // 2, LANES)) < 64

    def remote(src, dst, send, recv, peer):
        return pltpu.make_async_remote_copy(
            src_ref=src, dst_ref=dst, send_sem=send, recv_sem=recv,
            device_id=peer, device_id_type=pl.DeviceIdType.MESH,
        )

    def exchanges(k):
        return (
            remote(vecs.at[k], hx.at[k, 1], hsend.at[k, 0], hrecv.at[k, 0], near[0]),
            remote(vecs.at[k], hx.at[k, 0], hsend.at[k, 1], hrecv.at[k, 1], near[1]),
            remote(ypack.at[k, 0], hy.at[k, 1], hsend.at[k, 2], hrecv.at[k, 2], near[2]),
            remote(ypack.at[k, 1], hy.at[k, 0], hsend.at[k, 3], hrecv.at[k, 3], near[3]),
        )

    def publish(k, v):
        copies = exchanges(k)
        vecs[k] = v
        for copy in copies[:2]:
            copy.start()
        low, high = v[: DOF // 2], pltpu.roll(v[DOF // 2 :], 64, 1)
        ypack[k, 0] = jnp.where(half, low, high)
        ypack[k, 1] = jnp.where(half, high, low)
        for copy in copies[2:]:
            copy.start()
        return copies

    zero8 = jnp.zeros((8, LANES), F32)
    half8 = lane((8, LANES)) < 64

    def prepare(places):
        @pl.loop(0, DOF // 8)
        def _(quad):
            for step in range(4):
                t = 4 * quad + step
                at = pl.multiple_of(t * LANES, LANES)

                def face(f):
                    if f is None:
                        return zero8
                    return jnp.concatenate([raw[f, :, pl.ds(at, LANES)], raw[7 + f, :, pl.ds(at, LANES)]], axis=0)

                for place_ in places:
                    one, two = PAIRS[place_]
                    a, b = face(one), face(two)
                    b_f32[place_, pl.ds(2 * t, 8, stride=DOF), :] = jnp.where(half8, a, pltpu.roll(b, 64, 1))
                    b_f32[place_, pl.ds(2 * t + 1, 8, stride=DOF), :] = jnp.where(half8, pltpu.roll(a, 64, 1), b)

        for i, place_ in enumerate(places):
            high, mid, low = split(b_f32[place_])
            for part, value in enumerate((mid, high, low)):
                at = 2 * LANES * part + LANES * i
                b_parts[places[0] // 2, :, at : at + LANES] = value

    v = transpose_groups(first)
    pl.semaphore_wait(barrier, count)
    sends = [publish(0, v)]
    load.wait()
    prepare((0, 1))
    prepare((2, 3))

    def product(which, vectors):
        high, mid, low = split(jnp.concatenate(vectors, axis=0))
        both = jnp.concatenate([high, mid], axis=1)
        wide = dot(b_parts[which, :, : 4 * LANES], jnp.concatenate([both, both], axis=0))
        rest = dot(b_parts[which, :, 2 * LANES :], jnp.concatenate([low, high], axis=0))
        total = wide[:, :LANES] + wide[:, LANES:] + rest
        out = total[:DOF]
        for e in range(1, ELEMS):
            out = jnp.where(lanes // 16 == e, total[DOF * e : DOF * (e + 1)], out)
        return out

    known = [at_distance(d) for d in (1, 2, 4) if 2 * d <= max(ny, nz) // 2]
    at_cell = (lanes // 16) % 4
    zero = jnp.zeros((DOF, LANES), F32)
    for k in range(POWERS):
        z_low = jnp.where(at_cell == 0, 0.0, pltpu.roll(v, 16, 1))
        z_high = jnp.where(at_cell == 3, 0.0, pltpu.roll(v, LANES - 16, 1))
        inner = v + product(0, [v, z_low, z_high, zero])
        swapped = pltpu.roll(v, 64, 1)
        if k < len(known):
            for peer in known[k]:
                signal(word.at[k], peer)
        for copy in sends[k]:
            copy.wait_recv()
        x_low = jnp.where(me_x > 0, hx[k, 0], 0.0)
        x_high = jnp.where(me_x < gx - 1, hx[k, 1], 0.0)
        y_low = jnp.where(me_y > 0, hy[k, 0], 0.0)
        y_high = jnp.where(me_y < gy - 1, hy[k, 1], 0.0)
        own_low, own_high = swapped[: DOF // 2], swapped[DOF // 2 :]
        y_low = jnp.concatenate(
            [jnp.where(half, pltpu.roll(y_low, 64, 1), own_low), jnp.where(half, y_low, own_high)], axis=0
        )
        y_high = jnp.concatenate(
            [jnp.where(half, own_low, pltpu.roll(y_high, 64, 1)), jnp.where(half, own_high, y_high)], axis=0
        )
        outer = product(1, [x_low, x_high, y_low, y_high])
        if k < len(known):
            pl.semaphore_wait(word.at[k], len(known[k]))
        v = inner + outer
        if k < POWERS - 1:
            sends.append(publish(k + 1, v))
        else:
            vecs[POWERS] = v

    columns = transpose_arrays([vecs[k] for k in range(POWERS + 1)] + [zero] * (7 - POWERS))
    for e in range(ELEMS):
        u_ref[DOF * e : DOF * (e + 1), :] = columns[e]

    def all_bytes(buffer, n, sem):
        return pltpu.make_async_copy(buffer.at[pl.ds(0, n - 1)], buffer.at[pl.ds(0, n - 1)], sem)

    def add_up(buffer, n):
        total = buffer[0]
        for i in range(1, n):
            total = total + buffer[i]
        return total

    def one_pass(number, _):
        u = u_ref[...]
        gram = dot_exact(u, u, 0)[:COLS]
        def block(k, to):
            part = gram[RHS * k : RHS * (k + 1)]
            return pltpu.roll(part, (to - RHS * k) % LANES, 1) if (to - RHS * k) % LANES else part

        lane16 = lane((RHS, LANES))
        top = jnp.where(lane16 < 80, block(0, 0), block(2, 80))
        low = jnp.where(lane16 < 64, block(1, 0), jnp.where(lane16 < 96, block(3, 64), block(4, 96)))
        both = jnp.concatenate([top, low], axis=0)
        piece = 2 * RHS // n_g
        for i in range(n_g):
            packed[number, i] = both[piece * i : piece * (i + 1)]

        def start_all(n, me, mate, src, dst, sem):
            for d in sorted(range(1, n), key=lambda d: -min(d, n - d)):
                other = lax.rem(me + d, n)
                remote(src(other), dst, asend.at[number, sem], arecv.at[number, sem], mate(other)).start()

        start_all(n_g, me_g, mate_g, lambda i: packed.at[number, i], stage_a.at[number, me_g], 0)
        stage_a[number, me_g] = packed[number, me_g]
        all_bytes(stage_a.at[number], n_g, arecv.at[number, 0]).wait()
        sum_a[number] = add_up(stage_a.at[number], n_g)
        start_all(ny, at_y, mate_y, lambda i: sum_a.at[number], stage_b.at[number, at_y], 1)
        stage_b[number, at_y] = sum_a[number]
        all_bytes(stage_b.at[number], ny, arecv.at[number, 1]).wait()
        sum_b[number] = add_up(stage_b.at[number], ny)
        start_all(nz, at_z, mate_z, lambda i: sum_b.at[number], stage_c.at[number, at_z], 2)
        stage_c[number, at_z] = sum_b[number]
        all_bytes(stage_c.at[number], nz, arecv.at[number, 2]).wait()
        sum_c[number] = add_up(stage_c.at[number], nz)
        start_all(n_g, me_g, mate_g, lambda i: sum_c.at[number], gathered.at[number, me_g], 3)
        gathered[number, me_g] = sum_c[number]
        all_bytes(gathered.at[number], n_g, arecv.at[number, 3]).wait()

        both = jnp.concatenate([gathered[number, i] for i in range(n_g)], axis=0)
        top, low = both[:RHS], both[RHS:]
        blocks_of = (
            (top, 0, 80), (low, 0, 64), (top, 80, 48), (low, 64, 32), (low, 96, 16)
        )
        upper = []
        for k, (source, at, width) in enumerate(blocks_of):
            shift = (RHS * k - at) % LANES
            part = pltpu.roll(source, shift, 1) if shift else source
            upper.append(jnp.where((lane16 >= RHS * k) & (lane16 < COLS), part, 0.0))
        upper = jnp.concatenate(upper + [jnp.zeros((LANES - COLS, LANES), F32)], axis=0)
        r_, c_ = row((LANES, LANES)), lane((LANES, LANES))
        full = jnp.where(r_ // RHS <= c_ // RHS, upper, upper.T)
        factor, inverse = eliminate(full[:COLS])
        r_ref[number] = factor
        inverse = jnp.concatenate([inverse, jnp.zeros((LANES - COLS, LANES), F32)], axis=0)
        u_ref[...] = dot_exact(u, inverse.T)
        return 0

    lax.fori_loop(0, 2, one_pass, 0)

    pad = jnp.zeros((LANES - COLS, LANES), F32)
    factor = dot_exact(r_ref[1], jnp.concatenate([r_ref[0], pad], axis=0))
    factor_ref[...] = factor[:, :COLS]
    columns = transpose_arrays([u_ref[DOF * e : DOF * (e + 1), :] for e in range(ELEMS)])
    for k in range(POWERS + 1):
        out = transpose_groups(columns[k])
        for t in range(8):
            at = slice(LANES * t, LANES * (t + 1))
            basis_ref[k, 0, :, at] = out[8 * t : 8 * t + 4]
            basis_ref[k, 1, :, at] = out[8 * t + 4 : 8 * t + 8]

    for copies in sends:
        for copy in copies:
            copy.wait_send()
    for number in range(2):
        all_bytes(stage_a.at[number], n_g, asend.at[number, 0]).wait()
        all_bytes(stage_b.at[number], ny, asend.at[number, 1]).wait()
        all_bytes(stage_c.at[number], nz, asend.at[number, 2]).wait()
        all_bytes(gathered.at[number], n_g, asend.at[number, 3]).wait()


def on_device(sizes, rhs, blocks):
    ny, nz, nc, nx = sizes
    n_g = nx * nc
    piece = 2 * RHS // n_g
    faces = blocks.transpose(0, 1, 3, 2, 4).reshape(14, 4, DOF * DOF)
    vmem = pltpu.VMEM
    basis, factor = pl.pallas_call(
        functools.partial(kernel, sizes),
        out_shape=(
            jax.ShapeDtypeStruct((POWERS + 1, 2, 4, DOF * RHS), F32),
            jax.ShapeDtypeStruct((COLS, COLS), F32),
        ),
        in_specs=[pl.BlockSpec(memory_space=pltpu.VMEM), pl.BlockSpec(memory_space=pl.ANY)],
        out_specs=(pl.BlockSpec(memory_space=pltpu.VMEM),) * 2,
        scratch_shapes=[
            vmem((14, 4, DOF * DOF), F32),
            vmem((4, ELEMS * DOF, LANES), F32),
            vmem((2, ELEMS * DOF, 6 * LANES), BF16),
            vmem((POWERS + 1, DOF, LANES), F32),
            vmem((POWERS, 2, DOF // 2, LANES), F32),
            vmem((POWERS, 2, DOF, LANES), F32),
            vmem((POWERS, 2, DOF // 2, LANES), F32),
            vmem((ELEMS * DOF, LANES), F32),
            vmem((2, n_g, piece, LANES), F32),
            vmem((2, n_g, piece, LANES), F32),
            vmem((2, ny, piece, LANES), F32),
            vmem((2, nz, piece, LANES), F32),
            vmem((2, piece, LANES), F32),
            vmem((2, piece, LANES), F32),
            vmem((2, piece, LANES), F32),
            vmem((2, n_g, piece, LANES), F32),
            vmem((2, COLS, LANES), F32),
            pltpu.SemaphoreType.DMA((1,)),
            pltpu.SemaphoreType.DMA((POWERS, 4)),
            pltpu.SemaphoreType.DMA((POWERS, 4)),
            pltpu.SemaphoreType.DMA((2, 4)),
            pltpu.SemaphoreType.DMA((2, 4)),
            pltpu.SemaphoreType.REGULAR((POWERS,)),
        ],
        compiler_params=pltpu.CompilerParams(
            collective_id=0, has_side_effects=True, vmem_limit_bytes=53 * 1024 * 1024 + 256 * 1024
        ),
        name="krylov_qr",
    )(rhs.reshape(2, 4, DOF * RHS), faces)
    return basis.reshape(POWERS + 1, 1, 2, 4, DOF * RHS), factor


def solution(mesh):
    gx, gy = mesh.shape["gx"], mesh.shape["gy"]
    nz = 16 if gx >= 64 else 2
    return jax.shard_map(
        functools.partial(on_device, (gx // (2 * nz), nz, 2, gy)),
        mesh=mesh,
        in_specs=(P("gx", "gy", None, None), P("gx", "gy", None, None, None)),
        out_specs=(P(None, "gx", "gy", None, None), P()),
        check_vma=False,
    )
```

```python
import functools

import jax
import jax.numpy as jnp
from jax import lax
from jax.experimental import pallas as pl
from jax.experimental.pallas import tpu as pltpu
from jax.sharding import PartitionSpec as P

DOF = 64
RHS = 16
POWERS = 4
COLS = 80
ELEMS = 8
LANES = 128
PANEL = 16
LEAD = 3
LATE = POWERS + 1 - LEAD
F32 = jnp.float32
BF16 = jnp.bfloat16
PAIRS = ((0, 5), (6, None), (1, 2), (3, 4))


def lane(shape):
    return lax.broadcasted_iota(jnp.int32, shape, len(shape) - 1)


def row(shape):
    return lax.broadcasted_iota(jnp.int32, shape, 0)


def split(a):
    high = a.astype(BF16)
    rest = a - high.astype(F32)
    mid = rest.astype(BF16)
    low = (rest - mid.astype(F32)).astype(BF16)
    return high, mid, low


def dot(a, b, dims=((1,), (0,))):
    return lax.dot_general(a, b, (dims, ((), ())), preferred_element_type=F32)


def dot_exact(a, b, side=1):
    a_high, a_mid, a_low = split(a)
    b_high, b_mid, b_low = split(b)
    both = jnp.concatenate([b_high, b_mid], axis=1)
    dims = ((side,), (0,))
    wide = dot(jnp.concatenate([a_mid, a_high], axis=side), jnp.concatenate([both, both], axis=0), dims)
    rest = dot(jnp.concatenate([a_high, a_low], axis=side), jnp.concatenate([b_low, b_high], axis=0), dims)
    n = b.shape[1]
    return wide[:, :n] + wide[:, n:] + rest


def transpose_groups(a):
    rows, group = row(a.shape) % 8, lane(a.shape) // 16
    count = a.shape[0]
    for bit in (1, 2, 4):
        up = pltpu.roll(pltpu.roll(a, bit, 0), LANES - 16 * bit, 1)
        down = pltpu.roll(pltpu.roll(a, count - bit, 0), 16 * bit, 1)
        r, g = (rows // bit) % 2, (group // bit) % 2
        a = jnp.where(r == g, a, jnp.where(r == 1, up, down))
    return a


def transpose_arrays(arrays):
    group = lane((DOF, LANES)) // 16
    arrays = list(arrays)
    for bit in (1, 2, 4):
        g = (group // bit) % 2
        out = []
        for place in range(8):
            other = arrays[place ^ bit]
            here = arrays[place]
            if (place // bit) % 2:
                out.append(jnp.where(g == 1, here, pltpu.roll(other, LANES - 16 * bit, 1)))
            else:
                out.append(jnp.where(g == 0, here, pltpu.roll(other, 16 * bit, 1)))
        arrays = out
    return arrays


def pick(a, index):
    return a[index : index + 1, :]


def spread(a, index):
    return jnp.broadcast_to(a[:, index : index + 1], a.shape)


def stacked(rows):
    at = row((PANEL, LANES))
    out = jnp.broadcast_to(rows[0], (PANEL, LANES))
    for m in range(1, PANEL):
        out = jnp.where(at == m, rows[m], out)
    return out


def forward(column, below, later, r, corner, start):
    at = lane((PANEL, LANES))
    for j in range(PANEL):
        inv = lax.rsqrt(pick(column[j], j))
        r[j] = r[j] * inv
        scaled = column[j] * inv
        corner = jnp.where(at == start + j, scaled, corner)
        for m in range(j + 1, PANEL):
            s = pick(scaled, m)
            column[m] = column[m] - scaled * s
            r[m] = r[m] - s * r[j]
        if below is not None:
            below[j] = below[j] * inv
            for m in range(j + 1, PANEL):
                below[m] = below[m] - below[j] * pick(scaled, m)
            later = later - below[j] * r[j]
    return later, jnp.where(at <= row((PANEL, LANES)) + start, corner, 0.0)


def eliminate(full):
    later = full
    count = full.shape[0]
    upper, diagonal, inverse = [], [], []
    at = lane((PANEL, LANES))
    for start in range(0, count, PANEL):
        more = start + PANEL < count
        column = [spread(later[:PANEL], start + j) for j in range(PANEL)]
        below = [spread(later[PANEL:], start + j) for j in range(PANEL)] if more else None
        lanes = lane(later.shape)
        own = (lanes >= start) & (lanes < start + PANEL)
        later = jnp.where(own, (row(later.shape) + start == lanes).astype(F32), later)
        first, later = later[:PANEL], later[PANEL:]
        r = [pick(first, j) for j in range(PANEL)]
        later, corner = forward(column, below, later, r, jnp.zeros((PANEL, LANES), F32), start)
        rows = stacked(r)
        inverse.append(jnp.where(at < start + PANEL, rows, 0.0))
        upper.append(jnp.where(at >= start + PANEL, rows, 0.0))
        diagonal.append(corner)
    below = jnp.concatenate(diagonal + [jnp.zeros((LANES - count, LANES), F32)], axis=0)
    return jnp.concatenate(upper, axis=0) + below.T[:count], jnp.concatenate(inverse, axis=0)


def eliminate_row(a, w, w_t, k):
    start = PANEL * k
    at = lane((PANEL, LANES))
    own = (at >= start) & (at < start + PANEL)
    lead = dot_exact(a, w_t)
    placed = jnp.concatenate(
        [jnp.zeros((start, LANES), F32), lead, jnp.zeros((LANES - start - PANEL, LANES), F32)], axis=0
    )
    rest = a - dot_exact(lead, placed.T)
    first = jnp.where(own, (row((PANEL, LANES)) + start == at).astype(F32), -dot_exact(lead, w))
    column = [spread(rest, start + j) for j in range(PANEL)]
    r = [pick(first, j) for j in range(PANEL)]
    _, corner = forward(column, None, None, r, jnp.zeros((PANEL, LANES), F32), start)
    return lead + corner, jnp.where(at < start + PANEL, stacked(r), 0.0)


def kernel(sizes, rhs_ref, blocks_ref, basis_ref, factor_ref, raw, b_f32, b_parts, vecs, ypack, hx, hy,
           u_ref, packed, stage_a, stage_b, stage_c, sum_a, sum_b, sum_c, gathered,
           halves, other_half, late_sum, late_yx, late_z, late_both,
           load_sem, hsend, hrecv, asend, arecv, lsend, lrecv, word):
    ny, nz, nc, nx = sizes
    gx, gy = ny * nz * nc, nx
    me_x, me_y = lax.axis_index("gx"), lax.axis_index("gy")
    core, chip = lax.rem(me_x, nc), lax.div(me_x, nc)
    at_z, at_y = lax.rem(chip, nz), lax.div(chip, nz)

    def place(y, z, c, x):
        return {"gx": (y * nz + z) * nc + c, "gy": x}

    me_g = me_y * nc + core
    n_g = nx * nc

    def mate_g(i):
        return place(at_y, at_z, lax.rem(i, nc), lax.div(i, nc))

    def mate_y(i):
        return place(i, at_z, core, me_y)

    def mate_z(i):
        return place(at_y, i, core, me_y)

    me_yx, n_yx = at_y * nx + me_y, ny * nx

    groups = ((n_g, me_g, mate_g), (ny, at_y, mate_y), (nz, at_z, mate_z))
    near = (
        {"gx": lax.rem(me_x + gx - 1, gx), "gy": me_y},
        {"gx": lax.rem(me_x + 1, gx), "gy": me_y},
        {"gx": me_x, "gy": lax.rem(me_y + gy - 1, gy)},
        {"gx": me_x, "gy": lax.rem(me_y + 1, gy)},
    )

    load = pltpu.make_async_copy(blocks_ref, raw, load_sem.at[0])
    load.start()
    barrier = pltpu.get_barrier_semaphore()

    def signal(semaphore, peer):
        pl.semaphore_signal(semaphore, inc=1, device_id=peer, device_id_type=pl.DeviceIdType.MESH)

    def at_distance(d):
        peers = []
        for n, me, mate in groups[1:]:
            if 2 * d <= n:
                peers.append(mate(lax.rem(me + d, n)))
            if 2 * d < n:
                peers.append(mate(lax.rem(me + n - d, n)))
        return peers

    greeted = list(near) + at_distance(1)
    for peer in greeted:
        signal(barrier, peer)
    for d in range(1, n_g):
        signal(barrier, mate_g(lax.rem(me_g + d, n_g)))
    count = len(greeted) + n_g - 1

    flat_rhs = jnp.concatenate([rhs_ref[0], rhs_ref[1]], axis=0)
    first = jnp.concatenate([flat_rhs[:, LANES * t : LANES * (t + 1)] for t in range(8)], axis=0)
    lanes = lane((DOF, LANES))
    half = lane((DOF // 2, LANES)) < 64

    def remote(src, dst, send, recv, peer):
        return pltpu.make_async_remote_copy(
            src_ref=src, dst_ref=dst, send_sem=send, recv_sem=recv,
            device_id=peer, device_id_type=pl.DeviceIdType.MESH,
        )

    def exchanges(k):
        return (
            remote(vecs.at[k], hx.at[k, 1], hsend.at[k, 0], hrecv.at[k, 0], near[0]),
            remote(vecs.at[k], hx.at[k, 0], hsend.at[k, 1], hrecv.at[k, 1], near[1]),
            remote(ypack.at[k, 0], hy.at[k, 1], hsend.at[k, 2], hrecv.at[k, 2], near[2]),
            remote(ypack.at[k, 1], hy.at[k, 0], hsend.at[k, 3], hrecv.at[k, 3], near[3]),
        )

    def publish(k, v):
        copies = exchanges(k)
        vecs[k] = v
        for copy in copies[:2]:
            copy.start()
        low, high = v[: DOF // 2], pltpu.roll(v[DOF // 2 :], 64, 1)
        ypack[k, 0] = jnp.where(half, low, high)
        ypack[k, 1] = jnp.where(half, high, low)
        for copy in copies[2:]:
            copy.start()
        return copies

    zero8 = jnp.zeros((8, LANES), F32)
    half8 = lane((8, LANES)) < 64

    def prepare(places):
        @pl.loop(0, DOF // 8)
        def _(quad):
            for step in range(4):
                t = 4 * quad + step
                at = pl.multiple_of(t * LANES, LANES)

                def face(f):
                    if f is None:
                        return zero8
                    return jnp.concatenate([raw[f, :, pl.ds(at, LANES)], raw[7 + f, :, pl.ds(at, LANES)]], axis=0)

                for place_ in places:
                    one, two = PAIRS[place_]
                    a, b = face(one), face(two)
                    b_f32[place_, pl.ds(2 * t, 8, stride=DOF), :] = jnp.where(half8, a, pltpu.roll(b, 64, 1))
                    b_f32[place_, pl.ds(2 * t + 1, 8, stride=DOF), :] = jnp.where(half8, pltpu.roll(a, 64, 1), b)

        for i, place_ in enumerate(places):
            high, mid, low = split(b_f32[place_])
            for part, value in enumerate((mid, high, low)):
                at = 2 * LANES * part + LANES * i
                b_parts[places[0] // 2, :, at : at + LANES] = value

    v = transpose_groups(first)
    pl.semaphore_wait(barrier, count)
    sends = [publish(0, v)]
    load.wait()
    prepare((0, 1))
    prepare((2, 3))

    def product(which, vectors):
        high, mid, low = split(jnp.concatenate(vectors, axis=0))
        both = jnp.concatenate([high, mid], axis=1)
        wide = dot(b_parts[which, :, : 4 * LANES], jnp.concatenate([both, both], axis=0))
        rest = dot(b_parts[which, :, 2 * LANES :], jnp.concatenate([low, high], axis=0))
        total = wide[:, :LANES] + wide[:, LANES:] + rest
        out = total[:DOF]
        for e in range(1, ELEMS):
            out = jnp.where(lanes // 16 == e, total[DOF * e : DOF * (e + 1)], out)
        return out

    known = [at_distance(d) for d in (1, 2, 4)]
    at_cell = (lanes // 16) % 4
    zero = jnp.zeros((DOF, LANES), F32)
    def all_bytes(buffer, n, sem):
        return pltpu.make_async_copy(buffer.at[pl.ds(0, n - 1)], buffer.at[pl.ds(0, n - 1)], sem)

    def add_up(buffer, n):
        parts = [buffer[i] for i in range(n)]
        while len(parts) > 1:
            parts = [parts[i] + parts[i + 1] for i in range(0, len(parts), 2)]
        return parts[0]

    def far_first(i, n):
        return lax.rem(n // 2 + (1 - 2 * lax.rem(i, 2)) * lax.div(i, 2), n)

    piece = 2 * RHS // n_g

    def send_pieces(n, me, mate, src, dst, sem):
        number, stage = sem

        @pl.loop(1, n)
        def _(i):
            other = lax.rem(me + far_first(i, n), n)
            remote(src(other), dst, asend.at[number, stage], arecv.at[number, stage], mate(other)).start()

    def lead_0(number, gram):
        low = lane((2 * RHS, LANES)) < 64
        both = jnp.where(low, gram[: 2 * RHS], pltpu.roll(gram[2 * RHS : 4 * RHS], 64, 1))
        for i in range(n_g):
            packed[number, i] = both[piece * i : piece * (i + 1)]
        send_pieces(n_g, me_g, mate_g, lambda i: packed.at[number, i], stage_a.at[number, me_g], (number, 0))
        stage_a[number, me_g] = packed[number, me_g]

    def lead_1(number):
        all_bytes(stage_a.at[number], n_g, arecv.at[number, 0]).wait()
        sum_a[number] = add_up(stage_a.at[number], n_g)
        send_pieces(ny, at_y, mate_y, lambda i: sum_a.at[number], stage_b.at[number, at_y], (number, 1))
        stage_b[number, at_y] = sum_a[number]

    def lead_2(number):
        all_bytes(stage_b.at[number], ny, arecv.at[number, 1]).wait()
        sum_b[number] = add_up(stage_b.at[number], ny)
        send_pieces(nz, at_z, mate_z, lambda i: sum_b.at[number], stage_c.at[number, at_z], (number, 2))
        stage_c[number, at_z] = sum_b[number]

    def lead_3(number):
        all_bytes(stage_c.at[number], nz, arecv.at[number, 2]).wait()
        sum_c[number] = add_up(stage_c.at[number], nz)
        send_pieces(n_g, me_g, mate_g, lambda i: sum_c.at[number], gathered.at[number, me_g], (number, 3))
        gathered[number, me_g] = sum_c[number]

    def lead_4(number):
        all_bytes(gathered.at[number], n_g, arecv.at[number, 3]).wait()
        both = jnp.concatenate([gathered[number, i] for i in range(n_g)], axis=0)
        full = jnp.concatenate([both, pltpu.roll(both, 64, 1)], axis=0)[: LEAD * RHS]
        return jnp.where(lane(full.shape) < LEAD * RHS, full, 0.0)

    partner = place(at_y, at_z, nc - 1 - core, me_y)

    def to_partner(number, c, stage):
        if stage == 0:
            src, dst = halves.at[number, c, nc - 1 - core], other_half.at[number, c]
        else:
            src, dst = late_sum.at[number, c, 2], late_both.at[number, c, core]
        return remote(src, dst, lsend.at[number, c, stage], lrecv.at[number, c, stage], partner)

    def late_0(number, k, rows):
        c = k - LEAD
        halves[number, c, 0] = rows[:8]
        halves[number, c, 1] = rows[8:]
        to_partner(number, c, 0).start()

    def late_1(number, k):
        c = k - LEAD
        to_partner(number, c, 0).wait_recv()
        total = halves[number, c, core] + other_half[number, c]
        late_sum[number, c, 0] = total

        @pl.loop(0, n_yx - 1)
        def _(j):
            y = lax.rem(at_y + far_first(lax.div(j, nx) + 1, ny), ny)
            x = lax.rem(me_y + lax.rem(j, nx) + 1, nx)
            remote(
                late_sum.at[number, c, 0], late_yx.at[number, c, me_yx],
                lsend.at[number, c, 1], lrecv.at[number, c, 1], place(y, at_z, core, x),
            ).start()

        late_yx[number, c, me_yx] = total

    def late_2(number, k):
        c = k - LEAD
        all_bytes(late_yx.at[number, c], n_yx, lrecv.at[number, c, 1]).wait()
        total = add_up(late_yx.at[number, c], n_yx)
        late_sum[number, c, 1] = total

        @pl.loop(1, nz)
        def _(i):
            other = lax.rem(at_z + far_first(i, nz), nz)
            remote(
                late_sum.at[number, c, 1], late_z.at[number, c, at_z],
                lsend.at[number, c, 2], lrecv.at[number, c, 2], mate_z(other),
            ).start()

        late_z[number, c, at_z] = total

    def late_3(number, k):
        c = k - LEAD
        all_bytes(late_z.at[number, c], nz, lrecv.at[number, c, 2]).wait()
        total = add_up(late_z.at[number, c], nz)
        late_sum[number, c, 2] = total
        to_partner(number, c, 3).start()
        late_both[number, c, core] = total

    def late_4(number, k):
        c = k - LEAD
        to_partner(number, c, 3).wait_recv()
        return jnp.concatenate([late_both[number, c, 0], late_both[number, c, 1]], axis=0)

    def gram_of(number):
        u = u_ref[number]
        return dot_exact(u, u, 0)

    def gram_rows(number, k):
        return gram_of(number)[RHS * k : RHS * (k + 1)]

    u_lane = lane((ELEMS * DOF, LANES)) // RHS

    def add_column(k, v):
        for e in range(ELEMS):
            here = slice(DOF * e, DOF * (e + 1))
            shift = (RHS * (k - e)) % LANES
            turned = pltpu.roll(v, shift, 1) if shift else v
            u_ref[0, here] = jnp.where(lanes // RHS == k, turned, u_ref[0, here])

    for k in range(POWERS):
        z_low = jnp.where(at_cell == 0, 0.0, pltpu.roll(v, 16, 1))
        z_high = jnp.where(at_cell == 3, 0.0, pltpu.roll(v, LANES - 16, 1))
        inner = v + product(0, [v, z_low, z_high, zero])
        swapped = pltpu.roll(v, 64, 1)
        if k < len(known):
            for peer in known[k]:
                signal(word.at[k], peer)
        if k == LEAD - 1:
            columns = transpose_arrays([vecs[i] for i in range(LEAD)] + [zero] * (8 - LEAD))
            for e in range(ELEMS):
                u_ref[0, DOF * e : DOF * (e + 1), :] = columns[e]
            lead_0(0, gram_of(0))
        if k == LEAD:
            add_column(k, v)
            late_0(0, k, gram_rows(0, k))
            lead_1(0)
            late_1(0, k)
        for copy in sends[k]:
            copy.wait_recv()
        x_low = jnp.where(me_x > 0, hx[k, 0], 0.0)
        x_high = jnp.where(me_x < gx - 1, hx[k, 1], 0.0)
        y_low = jnp.where(me_y > 0, hy[k, 0], 0.0)
        y_high = jnp.where(me_y < gy - 1, hy[k, 1], 0.0)
        own_low, own_high = swapped[: DOF // 2], swapped[DOF // 2 :]
        y_low = jnp.concatenate(
            [jnp.where(half, pltpu.roll(y_low, 64, 1), own_low), jnp.where(half, y_low, own_high)], axis=0
        )
        y_high = jnp.concatenate(
            [jnp.where(half, own_low, pltpu.roll(y_high, 64, 1)), jnp.where(half, own_high, y_high)], axis=0
        )
        outer = product(1, [x_low, x_high, y_low, y_high])
        v = inner + outer
        if k < POWERS - 1:
            sends.append(publish(k + 1, v))
        if k < len(known):
            pl.semaphore_wait(word.at[k], len(known[k]))

    def padded(rows, start=0):
        parts = [rows, jnp.zeros((LANES - start - rows.shape[0], LANES), F32)]
        if start:
            parts.insert(0, jnp.zeros((start, LANES), F32))
        return jnp.concatenate(parts, axis=0)

    class Pass:
        pass

    passes = [Pass(), Pass()]

    def solve_lead(number):
        p = passes[number]
        p.r, w = eliminate(lead_4(number))
        p.w = padded(w)
        p.w_t = p.w.T
        p.l = None

    def apply_lead(number):
        return dot_exact(u_ref[number], passes[number].w_t)

    def solve_late(number, k):
        p = passes[number]
        l_k, w_k = eliminate_row(late_4(number, k), p.w, p.w_t, k)
        l_k = padded(l_k, RHS * k)
        p.l = l_k if p.l is None else p.l + l_k
        if k < POWERS:
            p.w = p.w + padded(w_k, RHS * k)
            p.w_t = p.w.T
        return dot_exact(u_ref[number], jnp.concatenate([w_k] * (LANES // RHS), axis=0).T)

    def next_lead():
        u_ref[1] = apply_lead(0)
        lead_0(1, gram_of(1))

    def next_late(k):
        q = solve_late(0, k)
        u_ref[1] = jnp.where(u_lane == k, q, u_ref[1])
        late_0(1, k, gram_rows(1, k))

    def factor_of(number):
        p = passes[number]
        return padded(p.r) + p.l.T

    def give(k, column):
        out = transpose_groups(column)
        for t in range(8):
            at = slice(LANES * t, LANES * (t + 1))
            basis_ref[k, 0, :, at] = out[8 * t : 8 * t + 4]
            basis_ref[k, 1, :, at] = out[8 * t + 4 : 8 * t + 8]

    def give_lead():
        q = apply_lead(1)
        columns = transpose_arrays([q[DOF * e : DOF * (e + 1), :] for e in range(ELEMS)])
        for k in range(LEAD):
            give(k, columns[k])

    def give_late(k):
        q = solve_late(1, k)
        column = q[:DOF]
        for e in range(1, ELEMS):
            column = jnp.where(lanes // RHS == e, q[DOF * e : DOF * (e + 1)], column)
        give(k, column)

    last, before = POWERS, POWERS - 1
    add_column(last, v)
    late_0(0, last, gram_rows(0, last))
    lead_2(0)
    late_1(0, last)
    late_2(0, before)
    lead_3(0)
    late_2(0, last)
    late_3(0, before)
    solve_lead(0)
    next_lead()
    next_late(before)
    late_3(0, last)
    late_1(1, before)
    lead_1(1)
    next_late(last)
    first_r = factor_of(0)
    late_1(1, last)
    lead_2(1)
    late_2(1, before)
    late_2(1, last)
    lead_3(1)
    late_3(1, before)
    solve_lead(1)
    late_3(1, last)
    give_late(before)
    give_late(last)
    factor_ref[...] = dot_exact(factor_of(1)[:COLS], first_r)[:, :COLS]
    give_lead()

    for copies in sends:
        for copy in copies:
            copy.wait_send()
    for number in range(2):
        all_bytes(stage_a.at[number], n_g, asend.at[number, 0]).wait()
        all_bytes(stage_b.at[number], ny, asend.at[number, 1]).wait()
        all_bytes(stage_c.at[number], nz, asend.at[number, 2]).wait()
        all_bytes(gathered.at[number], n_g, asend.at[number, 3]).wait()
        for c in range(LATE):
            to_partner(number, c, 0).wait_send()
            all_bytes(late_yx.at[number, c], n_yx, lsend.at[number, c, 1]).wait()
            all_bytes(late_z.at[number, c], nz, lsend.at[number, c, 2]).wait()
            to_partner(number, c, 3).wait_send()


def on_device(sizes, rhs, blocks):
    ny, nz, nc, nx = sizes
    n_g = nx * nc
    piece = 2 * RHS // n_g
    faces = blocks.transpose(0, 1, 3, 2, 4).reshape(14, 4, DOF * DOF)
    vmem = pltpu.VMEM
    basis, factor = pl.pallas_call(
        functools.partial(kernel, sizes),
        out_shape=(
            jax.ShapeDtypeStruct((POWERS + 1, 2, 4, DOF * RHS), F32),
            jax.ShapeDtypeStruct((COLS, COLS), F32),
        ),
        in_specs=[pl.BlockSpec(memory_space=pltpu.VMEM), pl.BlockSpec(memory_space=pl.ANY)],
        out_specs=(pl.BlockSpec(memory_space=pltpu.VMEM),) * 2,
        scratch_shapes=[
            vmem((14, 4, DOF * DOF), F32),
            vmem((4, ELEMS * DOF, LANES), F32),
            vmem((2, ELEMS * DOF, 6 * LANES), BF16),
            vmem((POWERS + 1, DOF, LANES), F32),
            vmem((POWERS, 2, DOF // 2, LANES), F32),
            vmem((POWERS, 2, DOF, LANES), F32),
            vmem((POWERS, 2, DOF // 2, LANES), F32),
            vmem((2, ELEMS * DOF, LANES), F32),
            vmem((2, n_g, piece, LANES), F32),
            vmem((2, n_g, piece, LANES), F32),
            vmem((2, ny, piece, LANES), F32),
            vmem((2, nz, piece, LANES), F32),
            vmem((2, piece, LANES), F32),
            vmem((2, piece, LANES), F32),
            vmem((2, piece, LANES), F32),
            vmem((2, n_g, piece, LANES), F32),
            vmem((2, LATE, 2, 8, LANES), F32),
            vmem((2, LATE, 8, LANES), F32),
            vmem((2, LATE, 3, 8, LANES), F32),
            vmem((2, LATE, ny * nx, 8, LANES), F32),
            vmem((2, LATE, nz, 8, LANES), F32),
            vmem((2, LATE, 2, 8, LANES), F32),
            pltpu.SemaphoreType.DMA((1,)),
            pltpu.SemaphoreType.DMA((POWERS, 4)),
            pltpu.SemaphoreType.DMA((POWERS, 4)),
            pltpu.SemaphoreType.DMA((2, 4)),
            pltpu.SemaphoreType.DMA((2, 4)),
            pltpu.SemaphoreType.DMA((2, LATE, 4)),
            pltpu.SemaphoreType.DMA((2, LATE, 4)),
            pltpu.SemaphoreType.REGULAR((POWERS,)),
        ],
        compiler_params=pltpu.CompilerParams(
            collective_id=0, has_side_effects=True, vmem_limit_bytes=53 * 1024 * 1024 + 256 * 1024
        ),
        name="krylov_qr",
    )(rhs.reshape(2, 4, DOF * RHS), faces)
    return basis.reshape(POWERS + 1, 1, 2, 4, DOF * RHS), factor


def solution(mesh):
    gx, gy = mesh.shape["gx"], mesh.shape["gy"]
    nz = 16 if gx >= 64 else 2
    return jax.shard_map(
        functools.partial(on_device, (gx // (2 * nz), nz, 2, gy)),
        mesh=mesh,
        in_specs=(P("gx", "gy", None, None), P("gx", "gy", None, None, None)),
        out_specs=(P(None, "gx", "gy", None, None), P()),
        check_vma=False,
    )
```

```python
import functools

import jax
import jax.numpy as jnp
from jax import lax
from jax.experimental import pallas as pl
from jax.experimental.pallas import tpu as pltpu
from jax.sharding import PartitionSpec as P

DOF = 64
RHS = 16
POWERS = 4
COLS = 80
ELEMS = 8
LANES = 128
PANEL = 16
LEAD = 3
CHUNKS = POWERS + 2 - LEAD
F32 = jnp.float32
BF16 = jnp.bfloat16
PAIRS = ((0, 5), (6, None), (1, 2), (3, 4))


def lane(shape):
    return lax.broadcasted_iota(jnp.int32, shape, len(shape) - 1)


def row(shape):
    return lax.broadcasted_iota(jnp.int32, shape, 0)


def split(a):
    high = a.astype(BF16)
    rest = a - high.astype(F32)
    mid = rest.astype(BF16)
    low = (rest - mid.astype(F32)).astype(BF16)
    return high, mid, low


def dot(a, b, dims=((1,), (0,))):
    return lax.dot_general(a, b, (dims, ((), ())), preferred_element_type=F32)


def dot_exact(a, b, side=1):
    a_high, a_mid, a_low = split(a)
    b_high, b_mid, b_low = split(b)
    both = jnp.concatenate([b_high, b_mid], axis=1)
    dims = ((side,), (0,))
    wide = dot(jnp.concatenate([a_mid, a_high], axis=side), jnp.concatenate([both, both], axis=0), dims)
    rest = dot(jnp.concatenate([a_high, a_low], axis=side), jnp.concatenate([b_low, b_high], axis=0), dims)
    n = b.shape[1]
    return wide[:, :n] + wide[:, n:] + rest


def transpose_groups(a):
    rows, group = row(a.shape) % 8, lane(a.shape) // 16
    count = a.shape[0]
    for bit in (1, 2, 4):
        up = pltpu.roll(pltpu.roll(a, bit, 0), LANES - 16 * bit, 1)
        down = pltpu.roll(pltpu.roll(a, count - bit, 0), 16 * bit, 1)
        r, g = (rows // bit) % 2, (group // bit) % 2
        a = jnp.where(r == g, a, jnp.where(r == 1, up, down))
    return a


def transpose_arrays(arrays):
    group = lane((DOF, LANES)) // 16
    arrays = list(arrays)
    for bit in (1, 2, 4):
        g = (group // bit) % 2
        out = []
        for place in range(8):
            other = arrays[place ^ bit]
            here = arrays[place]
            if (place // bit) % 2:
                out.append(jnp.where(g == 1, here, pltpu.roll(other, LANES - 16 * bit, 1)))
            else:
                out.append(jnp.where(g == 0, here, pltpu.roll(other, 16 * bit, 1)))
        arrays = out
    return arrays


def pick(a, index):
    return a[index : index + 1, :]


def spread(a, index):
    return jnp.broadcast_to(a[:, index : index + 1], a.shape)


def stacked(rows):
    at = row((PANEL, LANES))
    out = jnp.broadcast_to(rows[0], (PANEL, LANES))
    for m in range(1, PANEL):
        out = jnp.where(at == m, rows[m], out)
    return out


def forward(column, below, later, r, corner, start):
    at = lane((PANEL, LANES))
    for j in range(PANEL):
        inv = lax.rsqrt(pick(column[j], j))
        r[j] = r[j] * inv
        scaled = column[j] * inv
        corner = jnp.where(at == start + j, scaled, corner)
        for m in range(j + 1, PANEL):
            s = pick(scaled, m)
            column[m] = column[m] - scaled * s
            r[m] = r[m] - s * r[j]
        if below is not None:
            below[j] = below[j] * inv
            for m in range(j + 1, PANEL):
                below[m] = below[m] - below[j] * pick(scaled, m)
            later = later - below[j] * r[j]
    return later, jnp.where(at <= row((PANEL, LANES)) + start, corner, 0.0)


def eliminate(full):
    later = full
    count = full.shape[0]
    upper, diagonal, inverse = [], [], []
    at = lane((PANEL, LANES))
    for start in range(0, count, PANEL):
        more = start + PANEL < count
        column = [spread(later[:PANEL], start + j) for j in range(PANEL)]
        below = [spread(later[PANEL:], start + j) for j in range(PANEL)] if more else None
        lanes = lane(later.shape)
        own = (lanes >= start) & (lanes < start + PANEL)
        later = jnp.where(own, (row(later.shape) + start == lanes).astype(F32), later)
        first, later = later[:PANEL], later[PANEL:]
        r = [pick(first, j) for j in range(PANEL)]
        later, corner = forward(column, below, later, r, jnp.zeros((PANEL, LANES), F32), start)
        rows = stacked(r)
        inverse.append(jnp.where(at < start + PANEL, rows, 0.0))
        upper.append(jnp.where(at >= start + PANEL, rows, 0.0))
        diagonal.append(corner)
    below = jnp.concatenate(diagonal + [jnp.zeros((LANES - count, LANES), F32)], axis=0)
    return jnp.concatenate(upper, axis=0) + below.T[:count], jnp.concatenate(inverse, axis=0)


def eliminate_row(a, w, w_t, k):
    start = PANEL * k
    at = lane((PANEL, LANES))
    own = (at >= start) & (at < start + PANEL)
    lead = dot_exact(a, w_t)
    placed = jnp.concatenate(
        [jnp.zeros((start, LANES), F32), lead, jnp.zeros((LANES - start - PANEL, LANES), F32)], axis=0
    )
    rest = a - dot_exact(lead, placed.T)
    first = jnp.where(own, (row((PANEL, LANES)) + start == at).astype(F32), -dot_exact(lead, w))
    column = [spread(rest, start + j) for j in range(PANEL)]
    r = [pick(first, j) for j in range(PANEL)]
    _, corner = forward(column, None, None, r, jnp.zeros((PANEL, LANES), F32), start)
    return lead + corner, jnp.where(at < start + PANEL, stacked(r), 0.0)


def kernel(sizes, rhs_ref, blocks_ref, basis_ref, factor_ref, raw, b_f32, b_parts, vecs, ypack, hx, hy,
           u_ref, halves, other_half, sums, from_yx, from_z, whole,
           load_sem, hsend, hrecv, csend, crecv, word):
    ny, nz, nc, nx = sizes
    gx, gy = ny * nz * nc, nx
    me_x, me_y = lax.axis_index("gx"), lax.axis_index("gy")
    core, chip = lax.rem(me_x, nc), lax.div(me_x, nc)
    at_z, at_y = lax.rem(chip, nz), lax.div(chip, nz)

    def place(y, z, c, x):
        return {"gx": (y * nz + z) * nc + c, "gy": x}

    def mate_y(i):
        return place(i, at_z, core, me_y)

    def mate_z(i):
        return place(at_y, i, core, me_y)

    me_yx, n_yx = at_y * nx + me_y, ny * nx
    lines = ((ny, at_y, mate_y), (nz, at_z, mate_z))
    near = (
        {"gx": lax.rem(me_x + gx - 1, gx), "gy": me_y},
        {"gx": lax.rem(me_x + 1, gx), "gy": me_y},
        {"gx": me_x, "gy": lax.rem(me_y + gy - 1, gy)},
        {"gx": me_x, "gy": lax.rem(me_y + 1, gy)},
    )

    load = pltpu.make_async_copy(blocks_ref, raw, load_sem.at[0])
    load.start()
    barrier = pltpu.get_barrier_semaphore()

    def signal(semaphore, peer):
        pl.semaphore_signal(semaphore, inc=1, device_id=peer, device_id_type=pl.DeviceIdType.MESH)

    def at_distance(d):
        peers = []
        for n, me, mate in lines:
            if 2 * d <= n:
                peers.append(mate(lax.rem(me + d, n)))
            if 2 * d < n:
                peers.append(mate(lax.rem(me + n - d, n)))
        return peers

    known = [at_distance(d) for d in (1, 2, 4)]
    greeted = list(near) + known[0] + [{"gx": me_x, "gy": lax.rem(me_y + d, nx)} for d in range(2, nx - 1)]
    for peer in greeted:
        signal(barrier, peer)
    count = len(greeted)

    flat_rhs = jnp.concatenate([rhs_ref[0], rhs_ref[1]], axis=0)
    first = jnp.concatenate([flat_rhs[:, LANES * t : LANES * (t + 1)] for t in range(8)], axis=0)
    lanes = lane((DOF, LANES))
    half = lane((DOF // 2, LANES)) < 64

    def remote(src, dst, send, recv, peer):
        return pltpu.make_async_remote_copy(
            src_ref=src, dst_ref=dst, send_sem=send, recv_sem=recv,
            device_id=peer, device_id_type=pl.DeviceIdType.MESH,
        )

    def exchanges(k):
        return (
            remote(vecs.at[k], hx.at[k, 1], hsend.at[k, 0], hrecv.at[k, 0], near[0]),
            remote(vecs.at[k], hx.at[k, 0], hsend.at[k, 1], hrecv.at[k, 1], near[1]),
            remote(ypack.at[k, 0], hy.at[k, 1], hsend.at[k, 2], hrecv.at[k, 2], near[2]),
            remote(ypack.at[k, 1], hy.at[k, 0], hsend.at[k, 3], hrecv.at[k, 3], near[3]),
        )

    def publish(k, v):
        copies = exchanges(k)
        vecs[k] = v
        for copy in copies[:2]:
            copy.start()
        low, high = v[: DOF // 2], pltpu.roll(v[DOF // 2 :], 64, 1)
        ypack[k, 0] = jnp.where(half, low, high)
        ypack[k, 1] = jnp.where(half, high, low)
        for copy in copies[2:]:
            copy.start()
        return copies

    zero8 = jnp.zeros((8, LANES), F32)
    half8 = lane((8, LANES)) < 64

    def prepare(places):
        @pl.loop(0, DOF // 8)
        def _(quad):
            for step in range(4):
                t = 4 * quad + step
                at = pl.multiple_of(t * LANES, LANES)

                def face(f):
                    if f is None:
                        return zero8
                    return jnp.concatenate([raw[f, :, pl.ds(at, LANES)], raw[7 + f, :, pl.ds(at, LANES)]], axis=0)

                for place_ in places:
                    one, two = PAIRS[place_]
                    a, b = face(one), face(two)
                    b_f32[place_, pl.ds(2 * t, 8, stride=DOF), :] = jnp.where(half8, a, pltpu.roll(b, 64, 1))
                    b_f32[place_, pl.ds(2 * t + 1, 8, stride=DOF), :] = jnp.where(half8, pltpu.roll(a, 64, 1), b)

        for i, place_ in enumerate(places):
            high, mid, low = split(b_f32[place_])
            for part, value in enumerate((mid, high, low)):
                at = 2 * LANES * part + LANES * i
                b_parts[places[0] // 2, :, at : at + LANES] = value

    v = transpose_groups(first)
    pl.semaphore_wait(barrier, count)
    sends = [publish(0, v)]

    def tell(step):
        for peer in known[step]:
            signal(word.at[step], peer)

    def hear(step):
        pl.semaphore_wait(word.at[step], len(known[step]))

    tell(0)
    load.wait()
    prepare((0, 1))
    prepare((2, 3))

    def product(which, vectors):
        high, mid, low = split(jnp.concatenate(vectors, axis=0))
        both = jnp.concatenate([high, mid], axis=1)
        wide = dot(b_parts[which, :, : 4 * LANES], jnp.concatenate([both, both], axis=0))
        rest = dot(b_parts[which, :, 2 * LANES :], jnp.concatenate([low, high], axis=0))
        total = wide[:, :LANES] + wide[:, LANES:] + rest
        out = total[:DOF]
        for e in range(1, ELEMS):
            out = jnp.where(lanes // 16 == e, total[DOF * e : DOF * (e + 1)], out)
        return out

    at_cell = (lanes // 16) % 4
    zero = jnp.zeros((DOF, LANES), F32)
    def padded(rows, start=0):
        parts = [rows, jnp.zeros((LANES - start - rows.shape[0], LANES), F32)]
        if start:
            parts.insert(0, jnp.zeros((start, LANES), F32))
        return jnp.concatenate(parts, axis=0)

    def all_bytes(buffer, n, sem):
        return pltpu.make_async_copy(buffer.at[pl.ds(0, n - 1)], buffer.at[pl.ds(0, n - 1)], sem)

    def add_up(buffer, n):
        parts = [buffer[i] for i in range(n)]
        while len(parts) > 1:
            parts = [parts[i] + parts[i + 1] for i in range(0, len(parts), 2)]
        return parts[0]

    def far_first(i, n):
        return lax.rem(n // 2 + (1 - 2 * lax.rem(i, 2)) * lax.div(i, 2), n)

    partner = place(at_y, at_z, nc - 1 - core, me_y)

    def to_partner(number, c, stage):
        if stage == 0:
            src, dst = halves.at[number, c, nc - 1 - core], other_half.at[number, c]
        else:
            src, dst = sums.at[number, c, 2], whole.at[number, c, core]
        return remote(src, dst, csend.at[number, c, stage], crecv.at[number, c, stage], partner)

    def start_sum(number, c, rows):
        halves[number, c, 0] = rows[:8]
        halves[number, c, 1] = rows[8:]
        to_partner(number, c, 0).start()

    def over_yx(number, c):
        to_partner(number, c, 0).wait_recv()
        total = halves[number, c, core] + other_half[number, c]
        sums[number, c, 0] = total

        @pl.loop(0, n_yx - 1)
        def _(j):
            y = lax.rem(at_y + far_first(lax.div(j, nx) + 1, ny), ny)
            x = lax.rem(me_y + lax.rem(j, nx) + 1, nx)
            remote(
                sums.at[number, c, 0], from_yx.at[number, c, me_yx],
                csend.at[number, c, 1], crecv.at[number, c, 1], place(y, at_z, core, x),
            ).start()

        from_yx[number, c, me_yx] = total

    def over_z(number, c):
        all_bytes(from_yx.at[number, c], n_yx, crecv.at[number, c, 1]).wait()
        total = add_up(from_yx.at[number, c], n_yx)
        sums[number, c, 1] = total

        @pl.loop(1, nz)
        def _(i):
            other = lax.rem(at_z + far_first(i, nz), nz)
            remote(
                sums.at[number, c, 1], from_z.at[number, c, at_z],
                csend.at[number, c, 2], crecv.at[number, c, 2], mate_z(other),
            ).start()

        from_z[number, c, at_z] = total

    def share(number, c):
        all_bytes(from_z.at[number, c], nz, crecv.at[number, c, 2]).wait()
        total = add_up(from_z.at[number, c], nz)
        sums[number, c, 2] = total
        to_partner(number, c, 3).start()
        whole[number, c, core] = total

    def finish_sum(number, c):
        to_partner(number, c, 3).wait_recv()
        return jnp.concatenate([whole[number, c, 0], whole[number, c, 1]], axis=0)

    def gram_of(number):
        u = u_ref[number]
        return dot_exact(u, u, 0)

    lane16 = lane((RHS, LANES))

    def start_lead(number):
        gram = gram_of(number)
        one, two, three = gram[:RHS], gram[RHS : 2 * RHS], gram[2 * RHS : 3 * RHS]
        one, two = pltpu.roll(one, 5 * RHS, 1), pltpu.roll(two, 3 * RHS, 1)
        start_sum(number, 0, jnp.where(lane16 < 3 * RHS, three, jnp.where(lane16 < 5 * RHS, two, one)))

    def finish_lead(number):
        rows = finish_sum(number, 0)
        one = jnp.where(lane16 < RHS, pltpu.roll(rows, 3 * RHS, 1), 0.0)
        two = jnp.where(lane16 < 2 * RHS, pltpu.roll(rows, 5 * RHS, 1), 0.0)
        three = jnp.where(lane16 < 3 * RHS, rows, 0.0)
        lower = padded(jnp.concatenate([one, two, three], axis=0))
        at = row((LANES, LANES)) // RHS >= lane((LANES, LANES)) // RHS
        return jnp.where(at, lower, lower.T)[: LEAD * RHS]

    def start_row(number, k):
        start_sum(number, k - LEAD + 1, gram_of(number)[RHS * k : RHS * (k + 1)])

    u_lane = lane((ELEMS * DOF, LANES)) // RHS

    def add_column(k, v):
        for e in range(ELEMS):
            here = slice(DOF * e, DOF * (e + 1))
            shift = (RHS * (k - e)) % LANES
            turned = pltpu.roll(v, shift, 1) if shift else v
            u_ref[0, here] = jnp.where(lanes // RHS == k, turned, u_ref[0, here])

    for k in range(POWERS):
        z_low = jnp.where(at_cell == 0, 0.0, pltpu.roll(v, 16, 1))
        z_high = jnp.where(at_cell == 3, 0.0, pltpu.roll(v, LANES - 16, 1))
        inner = v + product(0, [v, z_low, z_high, zero])
        swapped = pltpu.roll(v, 64, 1)
        if k < len(known) - 1:
            hear(k)
            tell(k + 1)
        if k == LEAD - 1:
            columns = transpose_arrays([vecs[i] for i in range(LEAD)] + [zero] * (8 - LEAD))
            for e in range(ELEMS):
                u_ref[0, DOF * e : DOF * (e + 1), :] = columns[e]
            start_lead(0)
            over_yx(0, 0)
        if k == LEAD:
            add_column(k, v)
            start_row(0, k)
            over_yx(0, 1)
        for copy in sends[k]:
            copy.wait_recv()
        x_low = jnp.where(me_x > 0, hx[k, 0], 0.0)
        x_high = jnp.where(me_x < gx - 1, hx[k, 1], 0.0)
        y_low = jnp.where(me_y > 0, hy[k, 0], 0.0)
        y_high = jnp.where(me_y < gy - 1, hy[k, 1], 0.0)
        own_low, own_high = swapped[: DOF // 2], swapped[DOF // 2 :]
        y_low = jnp.concatenate(
            [jnp.where(half, pltpu.roll(y_low, 64, 1), own_low), jnp.where(half, y_low, own_high)], axis=0
        )
        y_high = jnp.concatenate(
            [jnp.where(half, own_low, pltpu.roll(y_high, 64, 1)), jnp.where(half, own_high, y_high)], axis=0
        )
        outer = product(1, [x_low, x_high, y_low, y_high])
        v = inner + outer
        if k < POWERS - 1:
            sends.append(publish(k + 1, v))
        if k == len(known) - 2:
            hear(k + 1)

    class Pass:
        pass

    passes = [Pass(), Pass()]

    def solve_lead(number):
        p = passes[number]
        p.r, w = eliminate(finish_lead(number))
        p.w = padded(w)
        p.w_t = p.w.T
        p.l = None

    def apply_lead(number):
        return dot_exact(u_ref[number], passes[number].w_t)

    def solve_late(number, k):
        p = passes[number]
        l_k, w_k = eliminate_row(finish_sum(number, k - LEAD + 1), p.w, p.w_t, k)
        l_k = padded(l_k, RHS * k)
        p.l = l_k if p.l is None else p.l + l_k
        if k < POWERS:
            p.w = p.w + padded(w_k, RHS * k)
            p.w_t = p.w.T
        return dot_exact(u_ref[number], jnp.concatenate([w_k] * (LANES // RHS), axis=0).T)

    def next_lead():
        u_ref[1] = apply_lead(0)
        start_lead(1)

    def next_late(k):
        q = solve_late(0, k)
        u_ref[1] = jnp.where(u_lane == k, q, u_ref[1])
        start_row(1, k)

    def factor_of(number):
        p = passes[number]
        return padded(p.r) + p.l.T

    def give(k, column):
        out = transpose_groups(column)
        for t in range(8):
            at = slice(LANES * t, LANES * (t + 1))
            basis_ref[k, 0, :, at] = out[8 * t : 8 * t + 4]
            basis_ref[k, 1, :, at] = out[8 * t + 4 : 8 * t + 8]

    def give_lead():
        q = apply_lead(1)
        columns = transpose_arrays([q[DOF * e : DOF * (e + 1), :] for e in range(ELEMS)])
        for k in range(LEAD):
            give(k, columns[k])

    def give_late(k):
        q = solve_late(1, k)
        column = q[:DOF]
        for e in range(1, ELEMS):
            column = jnp.where(lanes // RHS == e, q[DOF * e : DOF * (e + 1)], column)
        give(k, column)

    last, before = POWERS, POWERS - 1
    add_column(last, v)
    start_row(0, last)
    over_z(0, 0)
    over_yx(0, 2)
    over_z(0, 1)
    over_z(0, 2)
    share(0, 0)
    solve_lead(0)
    next_lead()
    share(0, 1)
    over_yx(1, 0)
    next_late(before)
    share(0, 2)
    over_yx(1, 1)
    next_late(last)
    first_r = factor_of(0)
    over_yx(1, 2)
    over_z(1, 0)
    over_z(1, 1)
    over_z(1, 2)
    share(1, 0)
    solve_lead(1)
    give_lead()
    share(1, 1)
    give_late(before)
    share(1, 2)
    give_late(last)
    factor_ref[...] = dot_exact(factor_of(1)[:COLS], first_r)[:, :COLS]

    for copies in sends:
        for copy in copies:
            copy.wait_send()
    for number in range(2):
        for c in range(CHUNKS):
            to_partner(number, c, 0).wait_send()
            all_bytes(from_yx.at[number, c], n_yx, csend.at[number, c, 1]).wait()
            all_bytes(from_z.at[number, c], nz, csend.at[number, c, 2]).wait()
            to_partner(number, c, 3).wait_send()


def on_device(sizes, rhs, blocks):
    ny, nz, nc, nx = sizes
    faces = blocks.transpose(0, 1, 3, 2, 4).reshape(14, 4, DOF * DOF)
    vmem = pltpu.VMEM
    basis, factor = pl.pallas_call(
        functools.partial(kernel, sizes),
        out_shape=(
            jax.ShapeDtypeStruct((POWERS + 1, 2, 4, DOF * RHS), F32),
            jax.ShapeDtypeStruct((COLS, COLS), F32),
        ),
        in_specs=[pl.BlockSpec(memory_space=pltpu.VMEM), pl.BlockSpec(memory_space=pl.ANY)],
        out_specs=(pl.BlockSpec(memory_space=pltpu.VMEM),) * 2,
        scratch_shapes=[
            vmem((14, 4, DOF * DOF), F32),
            vmem((4, ELEMS * DOF, LANES), F32),
            vmem((2, ELEMS * DOF, 6 * LANES), BF16),
            vmem((POWERS + 1, DOF, LANES), F32),
            vmem((POWERS, 2, DOF // 2, LANES), F32),
            vmem((POWERS, 2, DOF, LANES), F32),
            vmem((POWERS, 2, DOF // 2, LANES), F32),
            vmem((2, ELEMS * DOF, LANES), F32),
            vmem((2, CHUNKS, 2, 8, LANES), F32),
            vmem((2, CHUNKS, 8, LANES), F32),
            vmem((2, CHUNKS, 3, 8, LANES), F32),
            vmem((2, CHUNKS, ny * nx, 8, LANES), F32),
            vmem((2, CHUNKS, nz, 8, LANES), F32),
            vmem((2, CHUNKS, 2, 8, LANES), F32),
            pltpu.SemaphoreType.DMA((1,)),
            pltpu.SemaphoreType.DMA((POWERS, 4)),
            pltpu.SemaphoreType.DMA((POWERS, 4)),
            pltpu.SemaphoreType.DMA((2, CHUNKS, 4)),
            pltpu.SemaphoreType.DMA((2, CHUNKS, 4)),
            pltpu.SemaphoreType.REGULAR((POWERS,)),
        ],
        compiler_params=pltpu.CompilerParams(
            collective_id=0, has_side_effects=True, vmem_limit_bytes=53 * 1024 * 1024 + 256 * 1024
        ),
        name="krylov_qr",
    )(rhs.reshape(2, 4, DOF * RHS), faces)
    return basis.reshape(POWERS + 1, 1, 2, 4, DOF * RHS), factor


def solution(mesh):
    gx, gy = mesh.shape["gx"], mesh.shape["gy"]
    nz = 16 if gx >= 64 else 2
    return jax.shard_map(
        functools.partial(on_device, (gx // (2 * nz), nz, 2, gy)),
        mesh=mesh,
        in_specs=(P("gx", "gy", None, None), P("gx", "gy", None, None, None)),
        out_specs=(P(None, "gx", "gy", None, None), P()),
        check_vma=False,
    )
```

```python
import functools

import jax
import jax.numpy as jnp
from jax import lax
from jax.experimental import pallas as pl
from jax.experimental.pallas import tpu as pltpu
from jax.sharding import PartitionSpec as P

DOF = 64
RHS = 16
POWERS = 4
COLS = 80
ELEMS = 8
LANES = 128
PANEL = 16
LEAD = 3
CHUNKS = POWERS + 2 - LEAD
SENT = (8, 4, 5)
F32 = jnp.float32
BF16 = jnp.bfloat16
PAIRS = ((0, 5), (6, None), (1, 2), (3, 4))


def lane(shape):
    return lax.broadcasted_iota(jnp.int32, shape, len(shape) - 1)


def row(shape):
    return lax.broadcasted_iota(jnp.int32, shape, 0)


def split(a):
    high = a.astype(BF16)
    rest = a - high.astype(F32)
    mid = rest.astype(BF16)
    low = (rest - mid.astype(F32)).astype(BF16)
    return high, mid, low


def dot(a, b, dims=((1,), (0,))):
    return lax.dot_general(a, b, (dims, ((), ())), preferred_element_type=F32)


def dot_exact(a, b, side=1):
    a_high, a_mid, a_low = split(a)
    b_high, b_mid, b_low = split(b)
    both = jnp.concatenate([b_high, b_mid], axis=1)
    dims = ((side,), (0,))
    wide = dot(jnp.concatenate([a_mid, a_high], axis=side), jnp.concatenate([both, both], axis=0), dims)
    rest = dot(jnp.concatenate([a_high, a_low], axis=side), jnp.concatenate([b_low, b_high], axis=0), dims)
    n = b.shape[1]
    return wide[:, :n] + wide[:, n:] + rest


def transpose_groups(a):
    rows, group = row(a.shape) % 8, lane(a.shape) // 16
    count = a.shape[0]
    for bit in (1, 2, 4):
        up = pltpu.roll(pltpu.roll(a, bit, 0), LANES - 16 * bit, 1)
        down = pltpu.roll(pltpu.roll(a, count - bit, 0), 16 * bit, 1)
        r, g = (rows // bit) % 2, (group // bit) % 2
        a = jnp.where(r == g, a, jnp.where(r == 1, up, down))
    return a


def transpose_arrays(arrays):
    group = lane((DOF, LANES)) // 16
    arrays = list(arrays)
    for bit in (1, 2, 4):
        g = (group // bit) % 2
        out = []
        for place in range(8):
            other = arrays[place ^ bit]
            here = arrays[place]
            if (place // bit) % 2:
                out.append(jnp.where(g == 1, here, pltpu.roll(other, LANES - 16 * bit, 1)))
            else:
                out.append(jnp.where(g == 0, here, pltpu.roll(other, 16 * bit, 1)))
        arrays = out
    return arrays


def pick(a, index):
    return a[index : index + 1, :]


def spread(a, index):
    return jnp.broadcast_to(a[:, index : index + 1], a.shape)


def stacked(rows):
    at = row((PANEL, LANES))
    out = jnp.broadcast_to(rows[0], (PANEL, LANES))
    for m in range(1, PANEL):
        out = jnp.where(at == m, rows[m], out)
    return out


def forward(column, below, later, r, corner, start):
    at = lane((PANEL, LANES))
    for j in range(PANEL):
        inv = lax.rsqrt(pick(column[j], j))
        r[j] = r[j] * inv
        scaled = column[j] * inv
        corner = jnp.where(at == start + j, scaled, corner)
        for m in range(j + 1, PANEL):
            s = pick(scaled, m)
            column[m] = column[m] - scaled * s
            r[m] = r[m] - s * r[j]
        if below is not None:
            below[j] = below[j] * inv
            for m in range(j + 1, PANEL):
                below[m] = below[m] - below[j] * pick(scaled, m)
            later = later - below[j] * r[j]
    return later, jnp.where(at <= row((PANEL, LANES)) + start, corner, 0.0)


def eliminate(full):
    later = full
    count = full.shape[0]
    upper, diagonal, inverse = [], [], []
    at = lane((PANEL, LANES))
    for start in range(0, count, PANEL):
        more = start + PANEL < count
        column = [spread(later[:PANEL], start + j) for j in range(PANEL)]
        below = [spread(later[PANEL:], start + j) for j in range(PANEL)] if more else None
        lanes = lane(later.shape)
        own = (lanes >= start) & (lanes < start + PANEL)
        later = jnp.where(own, (row(later.shape) + start == lanes).astype(F32), later)
        first, later = later[:PANEL], later[PANEL:]
        r = [pick(first, j) for j in range(PANEL)]
        later, corner = forward(column, below, later, r, jnp.zeros((PANEL, LANES), F32), start)
        rows = stacked(r)
        inverse.append(jnp.where(at < start + PANEL, rows, 0.0))
        upper.append(jnp.where(at >= start + PANEL, rows, 0.0))
        diagonal.append(corner)
    below = jnp.concatenate(diagonal + [jnp.zeros((LANES - count, LANES), F32)], axis=0)
    return jnp.concatenate(upper, axis=0) + below.T[:count], jnp.concatenate(inverse, axis=0)


def eliminate_row(a, w, w_t, k):
    start = PANEL * k
    at = lane((PANEL, LANES))
    own = (at >= start) & (at < start + PANEL)
    lead = dot_exact(a, w_t)
    placed = jnp.concatenate(
        [jnp.zeros((start, LANES), F32), lead, jnp.zeros((LANES - start - PANEL, LANES), F32)], axis=0
    )
    rest = a - dot_exact(lead, placed.T)
    first = jnp.where(own, (row((PANEL, LANES)) + start == at).astype(F32), -dot_exact(lead, w))
    column = [spread(rest, start + j) for j in range(PANEL)]
    r = [pick(first, j) for j in range(PANEL)]
    _, corner = forward(column, None, None, r, jnp.zeros((PANEL, LANES), F32), start)
    return lead + corner, jnp.where(at < start + PANEL, stacked(r), 0.0)


def kernel(sizes, rhs_ref, blocks_ref, basis_ref, factor_ref, raw, b_f32, b_inner, b_y, b_x, vecs, ypack, hx, hy, u_ref,
           load_sem, hsend, hrecv, csend, crecv, word, *chunks):
    ny, nz, nc, nx = sizes
    gx, gy = ny * nz * nc, nx
    me_x, me_y = lax.axis_index("gx"), lax.axis_index("gy")
    core, chip = lax.rem(me_x, nc), lax.div(me_x, nc)
    at_z, at_y = lax.rem(chip, nz), lax.div(chip, nz)

    def place(y, z, c, x):
        return {"gx": (y * nz + z) * nc + c, "gy": x}

    def mate_y(i):
        return place(i, at_z, core, me_y)

    def mate_z(i):
        return place(at_y, i, core, me_y)

    me_yx, n_yx = at_y * nx + me_y, ny * nx
    lines = ((ny, at_y, mate_y), (nz, at_z, mate_z))
    near = (
        {"gx": lax.rem(me_x + gx - 1, gx), "gy": me_y},
        {"gx": lax.rem(me_x + 1, gx), "gy": me_y},
        {"gx": me_x, "gy": lax.rem(me_y + gy - 1, gy)},
        {"gx": me_x, "gy": lax.rem(me_y + 1, gy)},
    )

    load = pltpu.make_async_copy(blocks_ref, raw, load_sem.at[0])
    load.start()
    barrier = pltpu.get_barrier_semaphore()

    def signal(semaphore, peer):
        pl.semaphore_signal(semaphore, inc=1, device_id=peer, device_id_type=pl.DeviceIdType.MESH)

    def at_distance(d):
        peers = []
        for n, me, mate in lines:
            if 2 * d <= n:
                peers.append(mate(lax.rem(me + d, n)))
            if 2 * d < n:
                peers.append(mate(lax.rem(me + n - d, n)))
        return peers

    known = [at_distance(d) for d in (1, 2, 4)]
    greeted = list(near) + known[0] + [{"gx": me_x, "gy": lax.rem(me_y + d, nx)} for d in range(2, nx - 1)]
    for peer in greeted:
        signal(barrier, peer)
    count = len(greeted)

    flat_rhs = jnp.concatenate([rhs_ref[0], rhs_ref[1]], axis=0)
    first = jnp.concatenate([flat_rhs[:, LANES * t : LANES * (t + 1)] for t in range(8)], axis=0)
    lanes = lane((DOF, LANES))
    half = lane((DOF // 2, LANES)) < 64

    def remote(src, dst, send, recv, peer):
        return pltpu.make_async_remote_copy(
            src_ref=src, dst_ref=dst, send_sem=send, recv_sem=recv,
            device_id=peer, device_id_type=pl.DeviceIdType.MESH,
        )

    def exchanges(k):
        return (
            remote(vecs.at[k], hx.at[k, 1], hsend.at[k, 0], hrecv.at[k, 0], near[0]),
            remote(vecs.at[k], hx.at[k, 0], hsend.at[k, 1], hrecv.at[k, 1], near[1]),
            remote(ypack.at[k, 0], hy.at[k, 1], hsend.at[k, 2], hrecv.at[k, 2], near[2]),
            remote(ypack.at[k, 1], hy.at[k, 0], hsend.at[k, 3], hrecv.at[k, 3], near[3]),
        )

    def publish(k, v):
        copies = exchanges(k)
        vecs[k] = v
        for copy in copies[:2]:
            copy.start()
        low, high = v[: DOF // 2], pltpu.roll(v[DOF // 2 :], 64, 1)
        ypack[k, 0] = jnp.where(half, low, high)
        ypack[k, 1] = jnp.where(half, high, low)
        for copy in copies[2:]:
            copy.start()
        return copies

    zero8 = jnp.zeros((8, LANES), F32)
    half8 = lane((8, LANES)) < 64

    def prepare(places, parts_ref):
        @pl.loop(0, DOF // 8)
        def _(quad):
            for step in range(4):
                t = 4 * quad + step
                at = pl.multiple_of(t * LANES, LANES)

                def face(f):
                    if f is None:
                        return zero8
                    return jnp.concatenate([raw[f, :, pl.ds(at, LANES)], raw[7 + f, :, pl.ds(at, LANES)]], axis=0)

                for place_ in places:
                    one, two = PAIRS[place_]
                    a, b = face(one), face(two)
                    b_f32[place_, pl.ds(2 * t, 8, stride=DOF), :] = jnp.where(half8, a, pltpu.roll(b, 64, 1))
                    b_f32[place_, pl.ds(2 * t + 1, 8, stride=DOF), :] = jnp.where(half8, pltpu.roll(a, 64, 1), b)

        for i, place_ in enumerate(places):
            high, mid, low = split(b_f32[place_])
            for part, value in enumerate((mid, high, low)):
                at = LANES * (len(places) * part + i)
                parts_ref[:, at : at + LANES] = value

    v = transpose_groups(first)
    pl.semaphore_wait(barrier, count)
    sends = [publish(0, v)]

    def tell(step):
        for peer in known[step]:
            signal(word.at[step], peer)

    def hear(step):
        pl.semaphore_wait(word.at[step], len(known[step]))

    tell(0)
    load.wait()
    prepare((0, 1), b_inner)
    prepare((3,), b_y)
    prepare((2,), b_x)

    def product(parts_ref, vectors):
        high, mid, low = split(jnp.concatenate(vectors, axis=0))
        both = jnp.concatenate([high, mid], axis=1)
        width = parts_ref.shape[1] // 3
        wide = dot(parts_ref[:, : 2 * width], jnp.concatenate([both, both], axis=0))
        rest = dot(parts_ref[:, width:], jnp.concatenate([low, high], axis=0))
        total = wide[:, :LANES] + wide[:, LANES:] + rest
        out = total[:DOF]
        for e in range(1, ELEMS):
            out = jnp.where(lanes // 16 == e, total[DOF * e : DOF * (e + 1)], out)
        return out

    at_cell = (lanes // 16) % 4
    zero = jnp.zeros((DOF, LANES), F32)
    def padded(rows, start=0):
        parts = [rows, jnp.zeros((LANES - start - rows.shape[0], LANES), F32)]
        if start:
            parts.insert(0, jnp.zeros((start, LANES), F32))
        return jnp.concatenate(parts, axis=0)

    def all_bytes(buffer, n, sem):
        return pltpu.make_async_copy(buffer.at[pl.ds(0, n - 1)], buffer.at[pl.ds(0, n - 1)], sem)

    def add_up(buffer, n):
        parts = [buffer[i] for i in range(n)]
        while len(parts) > 1:
            parts = [parts[i] + parts[i + 1] for i in range(0, len(parts), 2)]
        return parts[0]

    def far_first(i, n):
        return lax.rem(n // 2 + (1 - 2 * lax.rem(i, 2)) * lax.div(i, 2), n)

    halves, other_half, sums, from_yx, from_z, whole = (chunks[CHUNKS * i : CHUNKS * (i + 1)] for i in range(6))
    row8, lane8 = row((8, LANES)), lane((8, LANES))

    def turn_rows(rows, shifts):
        out = rows
        for i, shift in enumerate(shifts):
            if shift % LANES:
                out = jnp.where(row8 == i, pltpu.roll(rows, shift % LANES, 1), out)
        return out

    def pack(c, rows):
        if SENT[c] == 8:
            return rows
        packed = jnp.where(lane8 < 64, rows, pltpu.roll(pltpu.roll(rows, 4, 0), 64, 1))[:4]
        if SENT[c] == 4:
            return packed
        turned = turn_rows(rows, [64 + RHS * i for i in range(8)])
        tail = jnp.sum(jnp.where(lane8 // RHS == row8, turned, 0.0), axis=0, keepdims=True)
        return jnp.concatenate([packed, tail], axis=0)

    def unpack(c, packed):
        if SENT[c] == 8:
            return packed
        twice = jnp.concatenate([packed[:4], packed[:4]], axis=0)
        rows = jnp.where(lane8 < 64, jnp.where(row8 < 4, twice, pltpu.roll(twice, 64, 1)), 0.0)
        if SENT[c] == 4:
            return rows
        tail = jnp.where(lane8 // RHS == row8, jnp.broadcast_to(packed[4:], (8, LANES)), 0.0)
        return rows + turn_rows(tail, [64 - RHS * i for i in range(8)])

    partner = place(at_y, at_z, nc - 1 - core, me_y)

    def to_partner(number, c, stage):
        if stage == 0:
            src, dst = halves[c].at[number, nc - 1 - core], other_half[c].at[number]
        else:
            src, dst = sums[c].at[number, 2], whole[c].at[number, core]
        return remote(src, dst, csend.at[number, c, stage], crecv.at[number, c, stage], partner)

    def start_sum(number, c, rows):
        halves[c][number, 0] = pack(c, rows[:8])
        halves[c][number, 1] = pack(c, rows[8:])
        to_partner(number, c, 0).start()

    def over_yx(number, c):
        to_partner(number, c, 0).wait_recv()
        total = halves[c][number, core] + other_half[c][number]
        sums[c][number, 0] = total

        @pl.loop(0, n_yx - 1)
        def _(j):
            y = lax.rem(at_y + far_first(lax.div(j, nx) + 1, ny), ny)
            x = lax.rem(me_y + lax.rem(j, nx) + 1, nx)
            remote(
                sums[c].at[number, 0], from_yx[c].at[number, me_yx],
                csend.at[number, c, 1], crecv.at[number, c, 1], place(y, at_z, core, x),
            ).start()

        from_yx[c][number, me_yx] = total

    def over_z(number, c):
        all_bytes(from_yx[c].at[number], n_yx, crecv.at[number, c, 1]).wait()
        total = add_up(from_yx[c].at[number], n_yx)
        sums[c][number, 1] = total

        @pl.loop(1, nz)
        def _(i):
            other = lax.rem(at_z + far_first(i, nz), nz)
            remote(
                sums[c].at[number, 1], from_z[c].at[number, at_z],
                csend.at[number, c, 2], crecv.at[number, c, 2], mate_z(other),
            ).start()

        from_z[c][number, at_z] = total

    def share(number, c):
        all_bytes(from_z[c].at[number], nz, crecv.at[number, c, 2]).wait()
        total = add_up(from_z[c].at[number], nz)
        sums[c][number, 2] = total
        to_partner(number, c, 3).start()
        whole[c][number, core] = total

    def finish_sum(number, c):
        to_partner(number, c, 3).wait_recv()
        return jnp.concatenate([unpack(c, whole[c][number, i]) for i in range(2)], axis=0)

    def gram_of(number):
        u = u_ref[number]
        return dot_exact(u, u, 0)

    lane16 = lane((RHS, LANES))

    def start_lead(number):
        gram = gram_of(number)
        one, two, three = gram[:RHS], gram[RHS : 2 * RHS], gram[2 * RHS : 3 * RHS]
        one, two = pltpu.roll(one, 5 * RHS, 1), pltpu.roll(two, 3 * RHS, 1)
        start_sum(number, 0, jnp.where(lane16 < 3 * RHS, three, jnp.where(lane16 < 5 * RHS, two, one)))

    def finish_lead(number):
        rows = finish_sum(number, 0)
        one = jnp.where(lane16 < RHS, pltpu.roll(rows, 3 * RHS, 1), 0.0)
        two = jnp.where(lane16 < 2 * RHS, pltpu.roll(rows, 5 * RHS, 1), 0.0)
        three = jnp.where(lane16 < 3 * RHS, rows, 0.0)
        lower = padded(jnp.concatenate([one, two, three], axis=0))
        at = row((LANES, LANES)) // RHS >= lane((LANES, LANES)) // RHS
        return jnp.where(at, lower, lower.T)[: LEAD * RHS]

    def start_row(number, k):
        start_sum(number, k - LEAD + 1, gram_of(number)[RHS * k : RHS * (k + 1)])

    u_lane = lane((ELEMS * DOF, LANES)) // RHS

    def add_column(k, v):
        for e in range(ELEMS):
            here = slice(DOF * e, DOF * (e + 1))
            shift = (RHS * (k - e)) % LANES
            turned = pltpu.roll(v, shift, 1) if shift else v
            u_ref[0, here] = jnp.where(lanes // RHS == k, turned, u_ref[0, here])

    for k in range(POWERS):
        z_low = jnp.where(at_cell == 0, 0.0, pltpu.roll(v, 16, 1))
        z_high = jnp.where(at_cell == 3, 0.0, pltpu.roll(v, LANES - 16, 1))
        inner = v + product(b_inner, [v, z_low, z_high, zero])
        swapped = pltpu.roll(v, 64, 1)
        if k < len(known) - 1:
            hear(k)
            tell(k + 1)
        if k == LEAD - 1:
            columns = transpose_arrays([vecs[i] for i in range(LEAD)] + [zero] * (8 - LEAD))
            for e in range(ELEMS):
                u_ref[0, DOF * e : DOF * (e + 1), :] = columns[e]
            start_lead(0)
            over_yx(0, 0)
        if k == LEAD:
            add_column(k, v)
            start_row(0, k)
            over_yx(0, 1)
        for copy in sends[k][2:]:
            copy.wait_recv()
        y_low = jnp.where(me_y > 0, hy[k, 0], 0.0)
        y_high = jnp.where(me_y < gy - 1, hy[k, 1], 0.0)
        own_low, own_high = swapped[: DOF // 2], swapped[DOF // 2 :]
        y_low = jnp.concatenate(
            [jnp.where(half, pltpu.roll(y_low, 64, 1), own_low), jnp.where(half, y_low, own_high)], axis=0
        )
        y_high = jnp.concatenate(
            [jnp.where(half, own_low, pltpu.roll(y_high, 64, 1)), jnp.where(half, own_high, y_high)], axis=0
        )
        inner = inner + product(b_y, [y_low, y_high])
        for copy in sends[k][:2]:
            copy.wait_recv()
        x_low = jnp.where(me_x > 0, hx[k, 0], 0.0)
        x_high = jnp.where(me_x < gx - 1, hx[k, 1], 0.0)
        v = inner + product(b_x, [x_low, x_high])
        if k < POWERS - 1:
            sends.append(publish(k + 1, v))
        if k == len(known) - 2:
            hear(k + 1)

    class Pass:
        pass

    passes = [Pass(), Pass()]

    def solve_lead(number):
        p = passes[number]
        p.r, w = eliminate(finish_lead(number))
        p.w = padded(w)
        p.w_t = p.w.T
        p.l = None

    def apply_lead(number):
        return dot_exact(u_ref[number], passes[number].w_t)

    def solve_late(number, k):
        p = passes[number]
        l_k, w_k = eliminate_row(finish_sum(number, k - LEAD + 1), p.w, p.w_t, k)
        l_k = padded(l_k, RHS * k)
        p.l = l_k if p.l is None else p.l + l_k
        if k < POWERS:
            p.w = p.w + padded(w_k, RHS * k)
            p.w_t = p.w.T
        return dot_exact(u_ref[number], jnp.concatenate([w_k] * (LANES // RHS), axis=0).T)

    def next_lead():
        u_ref[1] = apply_lead(0)
        start_lead(1)

    def next_late(k):
        q = solve_late(0, k)
        u_ref[1] = jnp.where(u_lane == k, q, u_ref[1])
        start_row(1, k)

    def factor_of(number):
        p = passes[number]
        return padded(p.r) + p.l.T

    def give(k, column):
        out = transpose_groups(column)
        for t in range(8):
            at = slice(LANES * t, LANES * (t + 1))
            basis_ref[k, 0, :, at] = out[8 * t : 8 * t + 4]
            basis_ref[k, 1, :, at] = out[8 * t + 4 : 8 * t + 8]

    def give_lead():
        q = apply_lead(1)
        columns = transpose_arrays([q[DOF * e : DOF * (e + 1), :] for e in range(ELEMS)])
        for k in range(LEAD):
            give(k, columns[k])

    def give_late(k):
        q = solve_late(1, k)
        column = q[:DOF]
        for e in range(1, ELEMS):
            column = jnp.where(lanes // RHS == e, q[DOF * e : DOF * (e + 1)], column)
        give(k, column)

    last, before = POWERS, POWERS - 1
    add_column(last, v)
    start_row(0, last)
    over_z(0, 0)
    over_yx(0, 2)
    over_z(0, 1)
    over_z(0, 2)
    share(0, 0)
    solve_lead(0)
    next_lead()
    share(0, 1)
    over_yx(1, 0)
    next_late(before)
    share(0, 2)
    over_yx(1, 1)
    next_late(last)
    first_r = factor_of(0)
    over_yx(1, 2)
    over_z(1, 0)
    over_z(1, 1)
    over_z(1, 2)
    share(1, 0)
    solve_lead(1)
    give_lead()
    share(1, 1)
    give_late(before)
    share(1, 2)
    give_late(last)
    factor_ref[...] = dot_exact(factor_of(1)[:COLS], first_r)[:, :COLS]

    for copies in sends:
        for copy in copies:
            copy.wait_send()
    for number in range(2):
        for c in range(CHUNKS):
            to_partner(number, c, 0).wait_send()
            all_bytes(from_yx[c].at[number], n_yx, csend.at[number, c, 1]).wait()
            all_bytes(from_z[c].at[number], nz, csend.at[number, c, 2]).wait()
            to_partner(number, c, 3).wait_send()


def hand_over(basis_ref, factor_ref, basis_out, factor_out, sems):
    copies = [
        pltpu.make_async_copy(basis_ref, basis_out, sems.at[0]),
        pltpu.make_async_copy(factor_ref, factor_out, sems.at[1]),
    ]
    for copy in copies:
        copy.start()
    for copy in copies:
        copy.wait()


def on_device(sizes, rhs, blocks):
    ny, nz, nc, nx = sizes
    faces = blocks.transpose(0, 1, 3, 2, 4).reshape(14, 4, DOF * DOF)
    vmem = pltpu.VMEM
    shapes = (
        jax.ShapeDtypeStruct((POWERS + 1, 2, 4, DOF * RHS), F32),
        jax.ShapeDtypeStruct((COLS, COLS), F32),
    )
    basis, factor = pl.pallas_call(
        functools.partial(kernel, sizes),
        out_shape=shapes,
        in_specs=[pl.BlockSpec(memory_space=pltpu.VMEM), pl.BlockSpec(memory_space=pl.ANY)],
        out_specs=(pl.BlockSpec(memory_space=pltpu.VMEM),) * 2,
        scratch_shapes=[
            vmem((14, 4, DOF * DOF), F32),
            vmem((4, ELEMS * DOF, LANES), F32),
            vmem((ELEMS * DOF, 6 * LANES), BF16),
            vmem((ELEMS * DOF, 3 * LANES), BF16),
            vmem((ELEMS * DOF, 3 * LANES), BF16),
            vmem((POWERS + 1, DOF, LANES), F32),
            vmem((POWERS, 2, DOF // 2, LANES), F32),
            vmem((POWERS, 2, DOF, LANES), F32),
            vmem((POWERS, 2, DOF // 2, LANES), F32),
            vmem((2, ELEMS * DOF, LANES), F32),
            pltpu.SemaphoreType.DMA((1,)),
            pltpu.SemaphoreType.DMA((POWERS, 4)),
            pltpu.SemaphoreType.DMA((POWERS, 4)),
            pltpu.SemaphoreType.DMA((2, CHUNKS, 4)),
            pltpu.SemaphoreType.DMA((2, CHUNKS, 4)),
            pltpu.SemaphoreType.REGULAR((POWERS,)),
        ]
        + [
            vmem(shape + (rows, LANES), F32)
            for shape in ((2, 2), (2,), (2, 3), (2, ny * nx), (2, nz), (2, 2))
            for rows in SENT
        ],
        compiler_params=pltpu.CompilerParams(
            collective_id=0, has_side_effects=True, vmem_limit_bytes=53 * 1024 * 1024 + 256 * 1024
        ),
        name="krylov_qr",
    )(rhs.reshape(2, 4, DOF * RHS), faces)
    basis, factor = pl.pallas_call(
        hand_over,
        out_shape=shapes,
        in_specs=[pl.BlockSpec(memory_space=pltpu.VMEM)] * 2,
        out_specs=(pl.BlockSpec(memory_space=pl.ANY),) * 2,
        scratch_shapes=[pltpu.SemaphoreType.DMA((2,))],
        name="hand_over",
    )(basis, factor)
    return basis.reshape(POWERS + 1, 1, 2, 4, DOF * RHS), factor


def solution(mesh):
    gx, gy = mesh.shape["gx"], mesh.shape["gy"]
    nz = 16 if gx >= 64 else 2
    return jax.shard_map(
        functools.partial(on_device, (gx // (2 * nz), nz, 2, gy)),
        mesh=mesh,
        in_specs=(P("gx", "gy", None, None), P("gx", "gy", None, None, None)),
        out_specs=(P(None, "gx", "gy", None, None), P()),
        check_vma=False,
    )
```

```python
import functools

import jax
import jax.numpy as jnp
from jax import lax
from jax.experimental import pallas as pl
from jax.experimental.pallas import tpu as pltpu
from jax.sharding import PartitionSpec as P

DOF = 64
RHS = 16
POWERS = 4
COLS = 80
ELEMS = 8
LANES = 128
PANEL = 16
LEAD = 3
CHUNKS = POWERS + 2 - LEAD
SENT = (8, 4, 5)
F32 = jnp.float32
BF16 = jnp.bfloat16
PAIRS = ((0, 5), (6, None), (1, 2), (3, 4))


def lane(shape):
    return lax.broadcasted_iota(jnp.int32, shape, len(shape) - 1)


def row(shape):
    return lax.broadcasted_iota(jnp.int32, shape, 0)


def split(a):
    high = a.astype(BF16)
    rest = a - high.astype(F32)
    mid = rest.astype(BF16)
    low = (rest - mid.astype(F32)).astype(BF16)
    return high, mid, low


def dot(a, b, dims=((1,), (0,))):
    return lax.dot_general(a, b, (dims, ((), ())), preferred_element_type=F32)


def dot_exact(a, b, side=1):
    a_high, a_mid, a_low = split(a)
    b_high, b_mid, b_low = split(b)
    both = jnp.concatenate([b_high, b_mid], axis=1)
    dims = ((side,), (0,))
    wide = dot(jnp.concatenate([a_mid, a_high], axis=side), jnp.concatenate([both, both], axis=0), dims)
    rest = dot(jnp.concatenate([a_high, a_low], axis=side), jnp.concatenate([b_low, b_high], axis=0), dims)
    n = b.shape[1]
    return wide[:, :n] + wide[:, n:] + rest


def transpose_groups(a):
    rows, group = row(a.shape) % 8, lane(a.shape) // 16
    count = a.shape[0]
    for bit in (1, 2, 4):
        up = pltpu.roll(pltpu.roll(a, bit, 0), LANES - 16 * bit, 1)
        down = pltpu.roll(pltpu.roll(a, count - bit, 0), 16 * bit, 1)
        r, g = (rows // bit) % 2, (group // bit) % 2
        a = jnp.where(r == g, a, jnp.where(r == 1, up, down))
    return a


def transpose_arrays(arrays):
    group = lane((DOF, LANES)) // 16
    arrays = list(arrays)
    for bit in (1, 2, 4):
        g = (group // bit) % 2
        out = []
        for place in range(8):
            other = arrays[place ^ bit]
            here = arrays[place]
            if (place // bit) % 2:
                out.append(jnp.where(g == 1, here, pltpu.roll(other, LANES - 16 * bit, 1)))
            else:
                out.append(jnp.where(g == 0, here, pltpu.roll(other, 16 * bit, 1)))
        arrays = out
    return arrays


def pick(a, index):
    return a[index : index + 1, :]


def spread(a, index):
    return jnp.broadcast_to(a[:, index : index + 1], a.shape)


def stacked(rows):
    at = row((PANEL, LANES))
    out = jnp.broadcast_to(rows[0], (PANEL, LANES))
    for m in range(1, PANEL):
        out = jnp.where(at == m, rows[m], out)
    return out


def forward(column, below, later, r, corner, start):
    at = lane((PANEL, LANES))
    for j in range(PANEL):
        inv = lax.rsqrt(pick(column[j], j))
        r[j] = r[j] * inv
        scaled = column[j] * inv
        corner = jnp.where(at == start + j, scaled, corner)
        for m in range(j + 1, PANEL):
            s = pick(scaled, m)
            column[m] = column[m] - scaled * s
            r[m] = r[m] - s * r[j]
        if below is not None:
            below[j] = below[j] * inv
            for m in range(j + 1, PANEL):
                below[m] = below[m] - below[j] * pick(scaled, m)
            later = later - below[j] * r[j]
    return later, jnp.where(at <= row((PANEL, LANES)) + start, corner, 0.0)


def eliminate(full):
    later = full
    count = full.shape[0]
    upper, diagonal, inverse = [], [], []
    at = lane((PANEL, LANES))
    for start in range(0, count, PANEL):
        more = start + PANEL < count
        column = [spread(later[:PANEL], start + j) for j in range(PANEL)]
        below = [spread(later[PANEL:], start + j) for j in range(PANEL)] if more else None
        lanes = lane(later.shape)
        own = (lanes >= start) & (lanes < start + PANEL)
        later = jnp.where(own, (row(later.shape) + start == lanes).astype(F32), later)
        first, later = later[:PANEL], later[PANEL:]
        r = [pick(first, j) for j in range(PANEL)]
        later, corner = forward(column, below, later, r, jnp.zeros((PANEL, LANES), F32), start)
        rows = stacked(r)
        inverse.append(jnp.where(at < start + PANEL, rows, 0.0))
        upper.append(jnp.where(at >= start + PANEL, rows, 0.0))
        diagonal.append(corner)
    below = jnp.concatenate(diagonal + [jnp.zeros((LANES - count, LANES), F32)], axis=0)
    return jnp.concatenate(upper, axis=0) + below.T[:count], jnp.concatenate(inverse, axis=0)


def eliminate_row(a, w, w_t, k):
    start = PANEL * k
    at = lane((PANEL, LANES))
    own = (at >= start) & (at < start + PANEL)
    lead = dot_exact(a, w_t)
    placed = jnp.concatenate(
        [jnp.zeros((start, LANES), F32), lead, jnp.zeros((LANES - start - PANEL, LANES), F32)], axis=0
    )
    rest = a - dot_exact(lead, placed.T)
    first = jnp.where(own, (row((PANEL, LANES)) + start == at).astype(F32), -dot_exact(lead, w))
    column = [spread(rest, start + j) for j in range(PANEL)]
    r = [pick(first, j) for j in range(PANEL)]
    _, corner = forward(column, None, None, r, jnp.zeros((PANEL, LANES), F32), start)
    return lead + corner, jnp.where(at < start + PANEL, stacked(r), 0.0)


def kernel(sizes, rhs_ref, blocks_ref, basis_ref, factor_ref, raw, b_f32, b_inner, b_y, b_x, vecs, ypack, hx, hy, u_ref,
           load_sem, hsend, hrecv, csend, crecv, word, *chunks):
    ny, nz, nc, nx = sizes
    gx, gy = ny * nz * nc, nx
    me_x, me_y = lax.axis_index("gx"), lax.axis_index("gy")
    core, chip = lax.rem(me_x, nc), lax.div(me_x, nc)
    at_z, at_y = lax.rem(chip, nz), lax.div(chip, nz)

    def place(y, z, c, x):
        return {"gx": (y * nz + z) * nc + c, "gy": x}

    def mate_y(i):
        return place(i, at_z, core, me_y)

    def mate_z(i):
        return place(at_y, i, core, me_y)

    me_yx, n_yx = at_y * nx + me_y, ny * nx
    lines = ((ny, at_y, mate_y), (nz, at_z, mate_z))
    near = (
        {"gx": lax.rem(me_x + gx - 1, gx), "gy": me_y},
        {"gx": lax.rem(me_x + 1, gx), "gy": me_y},
        {"gx": me_x, "gy": lax.rem(me_y + gy - 1, gy)},
        {"gx": me_x, "gy": lax.rem(me_y + 1, gy)},
    )

    load = pltpu.make_async_copy(blocks_ref, raw, load_sem.at[0])
    load.start()
    barrier = pltpu.get_barrier_semaphore()

    def signal(semaphore, peer):
        pl.semaphore_signal(semaphore, inc=1, device_id=peer, device_id_type=pl.DeviceIdType.MESH)

    def at_distance(d):
        peers = []
        for n, me, mate in lines:
            if 2 * d <= n:
                peers.append(mate(lax.rem(me + d, n)))
            if 2 * d < n:
                peers.append(mate(lax.rem(me + n - d, n)))
        return peers

    known = [at_distance(d) for d in (1, 2, 4)]
    greeted = list(near) + known[0] + [{"gx": me_x, "gy": lax.rem(me_y + d, nx)} for d in range(2, nx - 1)]
    for peer in greeted:
        signal(barrier, peer)
    count = len(greeted)

    flat_rhs = jnp.concatenate([rhs_ref[0], rhs_ref[1]], axis=0)
    first = jnp.concatenate([flat_rhs[:, LANES * t : LANES * (t + 1)] for t in range(8)], axis=0)
    lanes = lane((DOF, LANES))
    half = lane((DOF // 2, LANES)) < 64

    def remote(src, dst, send, recv, peer):
        return pltpu.make_async_remote_copy(
            src_ref=src, dst_ref=dst, send_sem=send, recv_sem=recv,
            device_id=peer, device_id_type=pl.DeviceIdType.MESH,
        )

    def exchanges(k):
        return (
            remote(vecs.at[k], hx.at[k, 1], hsend.at[k, 0], hrecv.at[k, 0], near[0]),
            remote(vecs.at[k], hx.at[k, 0], hsend.at[k, 1], hrecv.at[k, 1], near[1]),
            remote(ypack.at[k, 0], hy.at[k, 1], hsend.at[k, 2], hrecv.at[k, 2], near[2]),
            remote(ypack.at[k, 1], hy.at[k, 0], hsend.at[k, 3], hrecv.at[k, 3], near[3]),
        )

    def publish(k, v):
        copies = exchanges(k)
        vecs[k] = v
        for copy in copies[:2]:
            copy.start()
        low, high = v[: DOF // 2], pltpu.roll(v[DOF // 2 :], 64, 1)
        ypack[k, 0] = jnp.where(half, low, high)
        ypack[k, 1] = jnp.where(half, high, low)
        for copy in copies[2:]:
            copy.start()
        return copies

    zero8 = jnp.zeros((8, LANES), F32)
    half8 = lane((8, LANES)) < 64

    def prepare(places, parts_ref):
        @pl.loop(0, DOF // 8)
        def _(quad):
            for step in range(4):
                t = 4 * quad + step
                at = pl.multiple_of(t * LANES, LANES)

                def face(f):
                    if f is None:
                        return zero8
                    return jnp.concatenate([raw[f, :, pl.ds(at, LANES)], raw[7 + f, :, pl.ds(at, LANES)]], axis=0)

                for place_ in places:
                    one, two = PAIRS[place_]
                    a, b = face(one), face(two)
                    b_f32[place_, pl.ds(2 * t, 8, stride=DOF), :] = jnp.where(half8, a, pltpu.roll(b, 64, 1))
                    b_f32[place_, pl.ds(2 * t + 1, 8, stride=DOF), :] = jnp.where(half8, pltpu.roll(a, 64, 1), b)

        for i, place_ in enumerate(places):
            high, mid, low = split(b_f32[place_])
            for part, value in enumerate((mid, high, low)):
                at = LANES * (len(places) * part + i)
                parts_ref[:, at : at + LANES] = value

    v = transpose_groups(first)
    pl.semaphore_wait(barrier, count)
    sends = [publish(0, v)]

    def tell(step):
        for peer in known[step]:
            signal(word.at[step], peer)

    def hear(step):
        pl.semaphore_wait(word.at[step], len(known[step]))

    tell(0)
    load.wait()
    prepare((0, 1), b_inner)
    prepare((3,), b_y)
    prepare((2,), b_x)

    def product(parts_ref, vectors):
        high, mid, low = split(jnp.concatenate(vectors, axis=0))
        both = jnp.concatenate([high, mid], axis=1)
        width = parts_ref.shape[1] // 3
        wide = dot(parts_ref[:, : 2 * width], jnp.concatenate([both, both], axis=0))
        rest = dot(parts_ref[:, width:], jnp.concatenate([low, high], axis=0))
        total = wide[:, :LANES] + wide[:, LANES:] + rest
        out = total[:DOF]
        for e in range(1, ELEMS):
            out = jnp.where(lanes // 16 == e, total[DOF * e : DOF * (e + 1)], out)
        return out

    at_cell = (lanes // 16) % 4
    zero = jnp.zeros((DOF, LANES), F32)
    def padded(rows, start=0):
        parts = [rows, jnp.zeros((LANES - start - rows.shape[0], LANES), F32)]
        if start:
            parts.insert(0, jnp.zeros((start, LANES), F32))
        return jnp.concatenate(parts, axis=0)

    def all_bytes(buffer, n, sem):
        return pltpu.make_async_copy(buffer.at[pl.ds(0, n - 1)], buffer.at[pl.ds(0, n - 1)], sem)

    def add_up(buffer, n):
        parts = [buffer[i] for i in range(n)]
        while len(parts) > 1:
            parts = [parts[i] + parts[i + 1] for i in range(0, len(parts), 2)]
        return parts[0]

    def far_first(i, n):
        return lax.rem(n // 2 + (1 - 2 * lax.rem(i, 2)) * lax.div(i, 2), n)

    halves, other_half, sums, from_yx, from_z, whole = (chunks[CHUNKS * i : CHUNKS * (i + 1)] for i in range(6))
    row8, lane8 = row((8, LANES)), lane((8, LANES))

    def turn_rows(rows, shifts):
        out = rows
        for i, shift in enumerate(shifts):
            if shift % LANES:
                out = jnp.where(row8 == i, pltpu.roll(rows, shift % LANES, 1), out)
        return out

    def pack(c, rows):
        if SENT[c] == 8:
            return rows
        packed = jnp.where(lane8 < 64, rows, pltpu.roll(pltpu.roll(rows, 4, 0), 64, 1))[:4]
        if SENT[c] == 4:
            return packed
        turned = turn_rows(rows, [64 + RHS * i for i in range(8)])
        tail = jnp.sum(jnp.where(lane8 // RHS == row8, turned, 0.0), axis=0, keepdims=True)
        return jnp.concatenate([packed, tail], axis=0)

    def unpack(c, packed):
        if SENT[c] == 8:
            return packed
        twice = jnp.concatenate([packed[:4], packed[:4]], axis=0)
        rows = jnp.where(lane8 < 64, jnp.where(row8 < 4, twice, pltpu.roll(twice, 64, 1)), 0.0)
        if SENT[c] == 4:
            return rows
        tail = jnp.where(lane8 // RHS == row8, jnp.broadcast_to(packed[4:], (8, LANES)), 0.0)
        return rows + turn_rows(tail, [64 - RHS * i for i in range(8)])

    partner = place(at_y, at_z, nc - 1 - core, me_y)

    def to_partner(number, c, stage):
        if stage == 0:
            src, dst = halves[c].at[number, nc - 1 - core], other_half[c].at[number]
        else:
            src, dst = sums[c].at[number, 2], whole[c].at[number, core]
        return remote(src, dst, csend.at[number, c, stage], crecv.at[number, c, stage], partner)

    def start_sum(number, c, rows):
        halves[c][number, 0] = pack(c, rows[:8])
        halves[c][number, 1] = pack(c, rows[8:])
        to_partner(number, c, 0).start()

    def over_yx(number, c):
        to_partner(number, c, 0).wait_recv()
        total = halves[c][number, core] + other_half[c][number]
        sums[c][number, 0] = total

        @pl.loop(0, n_yx - 1)
        def _(j):
            y = lax.rem(at_y + far_first(lax.div(j, nx) + 1, ny), ny)
            x = lax.rem(me_y + lax.rem(j, nx) + 1, nx)
            remote(
                sums[c].at[number, 0], from_yx[c].at[number, me_yx],
                csend.at[number, c, 1], crecv.at[number, c, 1], place(y, at_z, core, x),
            ).start()

        from_yx[c][number, me_yx] = total

    def over_z(number, c):
        all_bytes(from_yx[c].at[number], n_yx, crecv.at[number, c, 1]).wait()
        total = add_up(from_yx[c].at[number], n_yx)
        sums[c][number, 1] = total

        @pl.loop(1, nz)
        def _(i):
            other = lax.rem(at_z + far_first(i, nz), nz)
            remote(
                sums[c].at[number, 1], from_z[c].at[number, at_z],
                csend.at[number, c, 2], crecv.at[number, c, 2], mate_z(other),
            ).start()

        from_z[c][number, at_z] = total

    def share(number, c):
        all_bytes(from_z[c].at[number], nz, crecv.at[number, c, 2]).wait()
        total = add_up(from_z[c].at[number], nz)
        sums[c][number, 2] = total
        to_partner(number, c, 3).start()
        whole[c][number, core] = total

    def finish_sum(number, c):
        to_partner(number, c, 3).wait_recv()
        return jnp.concatenate([unpack(c, whole[c][number, i]) for i in range(2)], axis=0)

    def gram_of(number):
        u = u_ref[number]
        return dot_exact(u, u, 0)

    lane16 = lane((RHS, LANES))

    def start_lead(number):
        gram = gram_of(number)
        one, two, three = gram[:RHS], gram[RHS : 2 * RHS], gram[2 * RHS : 3 * RHS]
        one, two = pltpu.roll(one, 5 * RHS, 1), pltpu.roll(two, 3 * RHS, 1)
        start_sum(number, 0, jnp.where(lane16 < 3 * RHS, three, jnp.where(lane16 < 5 * RHS, two, one)))

    def finish_lead(number):
        rows = finish_sum(number, 0)
        one = jnp.where(lane16 < RHS, pltpu.roll(rows, 3 * RHS, 1), 0.0)
        two = jnp.where(lane16 < 2 * RHS, pltpu.roll(rows, 5 * RHS, 1), 0.0)
        three = jnp.where(lane16 < 3 * RHS, rows, 0.0)
        lower = padded(jnp.concatenate([one, two, three], axis=0))
        at = row((LANES, LANES)) // RHS >= lane((LANES, LANES)) // RHS
        return jnp.where(at, lower, lower.T)[: LEAD * RHS]

    def start_row(number, k):
        start_sum(number, k - LEAD + 1, gram_of(number)[RHS * k : RHS * (k + 1)])

    def of_elements(q):
        column = q[:DOF]
        for e in range(1, ELEMS):
            column = jnp.where(lanes // RHS == e, q[DOF * e : DOF * (e + 1)], column)
        return column

    u_lane = lane((ELEMS * DOF, LANES)) // RHS

    def add_column(k, v):
        for e in range(ELEMS):
            here = slice(DOF * e, DOF * (e + 1))
            shift = (RHS * (k - e)) % LANES
            turned = pltpu.roll(v, shift, 1) if shift else v
            u_ref[0, here] = jnp.where(lanes // RHS == k, turned, u_ref[0, here])

    for k in range(POWERS):
        z_low = jnp.where(at_cell == 0, 0.0, pltpu.roll(v, 16, 1))
        z_high = jnp.where(at_cell == 3, 0.0, pltpu.roll(v, LANES - 16, 1))
        inner = v + product(b_inner, [v, z_low, z_high, zero])
        swapped = pltpu.roll(v, 64, 1)
        if k < len(known) - 1:
            hear(k)
            tell(k + 1)
        if k == LEAD - 1:
            columns = transpose_arrays([vecs[i] for i in range(LEAD)] + [zero] * (8 - LEAD))
            for e in range(ELEMS):
                u_ref[0, DOF * e : DOF * (e + 1), :] = columns[e]
            start_lead(0)
            over_yx(0, 0)
        if k == LEAD:
            add_column(k, v)
            start_row(0, k)
            over_yx(0, 1)
        for copy in sends[k][2:]:
            copy.wait_recv()
        y_low = jnp.where(me_y > 0, hy[k, 0], 0.0)
        y_high = jnp.where(me_y < gy - 1, hy[k, 1], 0.0)
        own_low, own_high = swapped[: DOF // 2], swapped[DOF // 2 :]
        y_low = jnp.concatenate(
            [jnp.where(half, pltpu.roll(y_low, 64, 1), own_low), jnp.where(half, y_low, own_high)], axis=0
        )
        y_high = jnp.concatenate(
            [jnp.where(half, own_low, pltpu.roll(y_high, 64, 1)), jnp.where(half, own_high, y_high)], axis=0
        )
        inner = inner + product(b_y, [y_low, y_high])
        for copy in sends[k][:2]:
            copy.wait_recv()
        x_low = jnp.where(me_x > 0, hx[k, 0], 0.0)
        x_high = jnp.where(me_x < gx - 1, hx[k, 1], 0.0)
        v = inner + product(b_x, [x_low, x_high])
        if k < POWERS - 1:
            sends.append(publish(k + 1, v))
        if k == len(known) - 2:
            hear(k + 1)

    class Pass:
        pass

    passes = [Pass(), Pass()]

    def solve_lead(number):
        p = passes[number]
        p.r, w = eliminate(finish_lead(number))
        p.w = padded(w)
        p.w_t = p.w.T
        p.l = None

    def apply_lead(number):
        return dot_exact(u_ref[number], passes[number].w_t)

    def solve_late(number, k):
        p = passes[number]
        l_k, w_k = eliminate_row(finish_sum(number, k - LEAD + 1), p.w, p.w_t, k)
        l_k = padded(l_k, RHS * k)
        p.l = l_k if p.l is None else p.l + l_k
        if k < POWERS:
            p.w = p.w + padded(w_k, RHS * k)
            p.w_t = p.w.T
        return dot_exact(u_ref[number], jnp.concatenate([w_k] * (LANES // RHS), axis=0).T)

    def next_lead():
        u_ref[1] = apply_lead(0)
        start_lead(1)

    def next_late(k):
        q = solve_late(0, k)
        u_ref[1] = jnp.where(u_lane == k, q, u_ref[1])
        start_row(1, k)

    def factor_of(number):
        p = passes[number]
        return padded(p.r) + p.l.T

    def give(k, column):
        out = transpose_groups(column)
        for t in range(8):
            at = slice(LANES * t, LANES * (t + 1))
            basis_ref[k, 0, :, at] = out[8 * t : 8 * t + 4]
            basis_ref[k, 1, :, at] = out[8 * t + 4 : 8 * t + 8]

    def give_lead():
        q = apply_lead(1)
        columns = transpose_arrays([q[DOF * e : DOF * (e + 1), :] for e in range(ELEMS)])
        for k in range(LEAD):
            give(k, columns[k])

    def give_late(k):
        give(k, of_elements(solve_late(1, k)))

    last, before = POWERS, POWERS - 1
    add_column(last, v)
    start_row(0, last)
    over_z(0, 0)
    over_yx(0, 2)
    over_z(0, 1)
    share(0, 0)
    over_z(0, 2)
    solve_lead(0)
    next_lead()
    share(0, 1)
    over_yx(1, 0)
    next_late(before)
    share(0, 2)
    over_yx(1, 1)
    next_late(last)
    over_z(1, 0)
    over_yx(1, 2)
    first_r = factor_of(0)
    over_z(1, 1)
    over_z(1, 2)
    share(1, 0)
    solve_lead(1)
    share(1, 1)
    give_late(before)
    give_lead()
    share(1, 2)
    give_late(last)
    factor_ref[...] = dot_exact(factor_of(1)[:COLS], first_r)[:, :COLS]

    for copies in sends:
        for copy in copies:
            copy.wait_send()
    for number in range(2):
        for c in range(CHUNKS):
            to_partner(number, c, 0).wait_send()
            all_bytes(from_yx[c].at[number], n_yx, csend.at[number, c, 1]).wait()
            all_bytes(from_z[c].at[number], nz, csend.at[number, c, 2]).wait()
            to_partner(number, c, 3).wait_send()


def on_device(sizes, rhs, blocks):
    ny, nz, nc, nx = sizes
    faces = blocks.transpose(0, 1, 3, 2, 4).reshape(14, 4, DOF * DOF)
    vmem = pltpu.VMEM
    shapes = (
        jax.ShapeDtypeStruct((POWERS + 1, 2, 4, DOF * RHS), F32),
        jax.ShapeDtypeStruct((COLS, COLS), F32),
    )
    basis, factor = pl.pallas_call(
        functools.partial(kernel, sizes),
        out_shape=shapes,
        in_specs=[pl.BlockSpec(memory_space=pltpu.VMEM), pl.BlockSpec(memory_space=pl.ANY)],
        out_specs=(pl.BlockSpec(memory_space=pltpu.VMEM),) * 2,
        scratch_shapes=[
            vmem((14, 4, DOF * DOF), F32),
            vmem((4, ELEMS * DOF, LANES), F32),
            vmem((ELEMS * DOF, 6 * LANES), BF16),
            vmem((ELEMS * DOF, 3 * LANES), BF16),
            vmem((ELEMS * DOF, 3 * LANES), BF16),
            vmem((POWERS + 1, DOF, LANES), F32),
            vmem((POWERS, 2, DOF // 2, LANES), F32),
            vmem((POWERS, 2, DOF, LANES), F32),
            vmem((POWERS, 2, DOF // 2, LANES), F32),
            vmem((2, ELEMS * DOF, LANES), F32),
            pltpu.SemaphoreType.DMA((1,)),
            pltpu.SemaphoreType.DMA((POWERS, 4)),
            pltpu.SemaphoreType.DMA((POWERS, 4)),
            pltpu.SemaphoreType.DMA((2, CHUNKS, 4)),
            pltpu.SemaphoreType.DMA((2, CHUNKS, 4)),
            pltpu.SemaphoreType.REGULAR((POWERS,)),
        ]
        + [
            vmem(shape + (rows, LANES), F32)
            for shape in ((2, 2), (2,), (2, 3), (2, ny * nx), (2, nz), (2, 2))
            for rows in SENT
        ],
        compiler_params=pltpu.CompilerParams(
            collective_id=0, has_side_effects=True, vmem_limit_bytes=53 * 1024 * 1024 + 256 * 1024
        ),
        name="krylov_qr",
    )(rhs.reshape(2, 4, DOF * RHS), faces)
    return basis.reshape(POWERS + 1, 1, 2, 4, DOF * RHS), factor


def solution(mesh):
    gx, gy = mesh.shape["gx"], mesh.shape["gy"]
    nz = 16 if gx >= 64 else 2
    return jax.shard_map(
        functools.partial(on_device, (gx // (2 * nz), nz, 2, gy)),
        mesh=mesh,
        in_specs=(P("gx", "gy", None, None), P("gx", "gy", None, None, None)),
        out_specs=(P(None, "gx", "gy", None, None), P()),
        check_vma=False,
    )
```
